256 devices in a mesh: chan: 64 (over x_lo, y, z), tm: 4 (over x_hi, core).
Axes of the slice: x: 4 (x_hi: 2, x_lo: 2; x = x_hi * 2 + x_lo), y: 4, z: 8, core: 2. Of those that a mesh axis runs over, the one named last changes fastest.
Arguments:
- samples: bfloat16 [1024, 2, 16, 16384], P('chan', None, 'tm'), may hold values from -6 to 6
- filter_taps: float32 [4, 16384], replicated, may hold values from -3 to 3
Outputs:
- visibility: float32 [64, 1024, 2048], P('chan', 'tm')
The draws below stay inside these ranges and needn't reach their ends.
All inputs are finite; a program needn't handle non-finite values.
Results may differ from the reference program's by a relative error of at most 0.01.
Values may be sent and summed in bfloat16 or wider, within the bound.
A program may use at most 128 MiB of HBM per device.

```python
import math
import jax
import jax.numpy as jnp
from jax import lax

INPUTS = 1024
F = 16384
ROOT = 128
TAPS = 4
SPEC_DEV = 4
SPECTRA = 16
BINS = 64
BIN = 256
N_TM = 4


def block_scale(rng, dims, shards, smallest, high):
    loudness, own = 1.0, jax.random.fold_in(rng, 6)
    for dim, blocks in shards:
        draws = jnp.exp(jax.random.uniform(jax.random.fold_in(own, dim), (blocks,), jnp.float32, smallest / len(shards), high / len(shards)))
        loudness = loudness * jnp.repeat(draws, dims[dim] // blocks).reshape([-1 if axis == dim else 1 for axis in range(len(dims))])
    return loudness


def centred(rng, extent, spread, most, cuts=(), kind=jnp.bfloat16):
    array = spread * jax.random.normal(rng, extent, jnp.float32)
    if cuts:
        array = array * block_scale(rng, extent, cuts, -0.22, 0.18)
    return jnp.clip(array, -most, most).astype(kind)


def setup_inputs(seed: int = 0) -> dict:
    key_of = jax.random.split(jax.random.key(seed), 3)
    samples = centred(key_of[0], (INPUTS, 2, SPECTRA, F), 1.0, 6.0, ((0, 64), (2, 4)))
    filter_taps = centred(key_of[1], (TAPS, F), 0.5, 3.0, (), jnp.float32)
    return dict(samples=samples, filter_taps=filter_taps)


def dft_tables(length):
    indices = jnp.arange(length, dtype=jnp.int32)
    product = (indices[:, None] * indices[None, :]) % length
    angles = product.astype(jnp.float32) * (2.0 * math.pi / length)
    cosine = jnp.cos(angles)
    sines_table = jnp.sin(angles)
    upper = jnp.stack([cosine, sines_table], axis=1)
    lower = jnp.stack([-sines_table, cosine], axis=1)
    return jnp.stack([upper, lower], axis=0).astype(jnp.bfloat16)


def channelize(window, filter_taps, number):
    filtered = filter_taps[0][None, None, None, :] * window[:, :, 0:number].astype(jnp.float32)
    for tap_index in range(1, TAPS):
        filtered = filtered + filter_taps[tap_index][None, None, None, :] * window[:, :, tap_index:tap_index + number].astype(jnp.float32)
    filtered = filtered.astype(jnp.bfloat16).reshape(window.shape[0], 2, number, ROOT, ROOT)
    matrix = dft_tables(ROOT)
    first_pass = jnp.einsum('pcra,irsab->ipscb', matrix.astype(jnp.float32), filtered.astype(jnp.float32))
    indices = jnp.arange(ROOT, dtype=jnp.int32)
    product = (indices[:, None] * indices[None, :]) % (ROOT * ROOT)
    angles = product.astype(jnp.float32) * (2.0 * math.pi / (ROOT * ROOT))
    cosine = jnp.cos(angles)
    sines_table = jnp.sin(angles)
    real_part = first_pass[:, 0]
    imag_part = first_pass[:, 1]
    twisted = jnp.stack([(real_part * cosine + imag_part * sines_table) / ROOT, (imag_part * cosine - real_part * sines_table) / ROOT], axis=1).astype(jnp.bfloat16)
    spectra = jnp.einsum('pdqb,iqscb->ipsdc', matrix.astype(jnp.float32), twisted.astype(jnp.float32))
    return spectra.astype(jnp.bfloat16)


def hermitian_operands(member):
    flattened = member.reshape(member.shape[0], -1)
    swapped = jnp.concatenate([-member[:, 1:2], member[:, 0:1]], axis=1).reshape(member.shape[0], -1)
    return flattened, jnp.concatenate([flattened, swapped], axis=0)


def correlate(row_side, col_side, factor):
    product = lax.dot_general(row_side.astype(jnp.float32), col_side.astype(jnp.float32), (((1,), (1,)), ((), ())))
    rounded = lax.optimization_barrier((product * factor).astype(jnp.bfloat16))
    return rounded.astype(jnp.float32)


def reference(samples, filter_taps):
    padded = jnp.concatenate([jnp.zeros((samples.shape[0], 2, TAPS - 1, F), jnp.bfloat16), samples], axis=2)

    def per_spectrum(position):
        window = lax.dynamic_slice_in_dim(padded, position, TAPS, 2)
        return channelize(window, filter_taps, 1)[:, :, 0]

    spectra = lax.map(per_spectrum, jnp.arange(SPECTRA, dtype=jnp.int32))
    per_bin = ROOT // BINS
    factor = 1.0 / (SPECTRA * BIN)

    def per_bin_fn(bin_index):
        chosen = lax.dynamic_slice_in_dim(spectra, bin_index * per_bin, per_bin, 3)
        total = jnp.zeros((INPUTS, 2 * INPUTS), jnp.float32)
        for time_block in range(N_TM):
            member = chosen[time_block * SPEC_DEV:(time_block + 1) * SPEC_DEV].transpose(1, 2, 0, 3, 4)
            row_side, col_side = hermitian_operands(member)
            total = total + correlate(row_side, col_side, factor)
        return total

    return lax.map(per_bin_fn, jnp.arange(BINS, dtype=jnp.int32))
```

```python
import functools
import math

import jax
import jax.numpy as jnp
import numpy as np
from jax import lax
from jax.experimental import pallas as pl
from jax.experimental.pallas import tpu as pltpu
from jax.sharding import PartitionSpec as P

ROOT = 128
TAPS = 4
SPEC = 4
INP = 16
MESH = pl.DeviceIdType.MESH
BF = jnp.bfloat16
F32 = jnp.float32


def dft_table():
    indices = np.arange(ROOT)
    angles = (indices[:, None] * indices[None, :] % ROOT) * (2.0 * math.pi / ROOT)
    cosine, sine = np.cos(angles), np.sin(angles)
    upper = np.concatenate([cosine, sine], axis=1)
    lower = np.concatenate([-sine, cosine], axis=1)
    return np.concatenate([upper, lower], axis=0)


def twiddle_table():
    indices = np.arange(ROOT)
    angles = (indices[:, None] * indices[None, :]) * (2.0 * math.pi / (ROOT * ROOT))
    return np.stack([np.cos(angles), np.sin(angles)]) / ROOT


def place():
    chan, tm = lax.axis_index("chan"), lax.axis_index("tm")
    return chan // 32, (chan // 8) % 4, chan % 8, tm


def turn_kernel(
    x_ref, taps_ref, m_ref, tw_ref, out_ref,
    xin, wide, frames, turned, snd, mid,
    in_sem, halo_s, halo_r, z_s, z_r, xy_s, xy_r, loc_sem,
):
    x_lo, y, z, tm = place()
    xy = x_lo * 4 + y

    def chan_of(xy_, z_):
        return xy_ * 8 + z_

    def other_xy(k):
        return ((x_lo + k // 4) % 2) * 4 + (y + k % 4) % 4

    for i in range(INP):
        pltpu.make_async_copy(x_ref.at[i], xin.at[i], in_sem.at[i]).start()

    barrier = pltpu.get_barrier_semaphore()
    for k in range(1, 8):
        pl.semaphore_signal(barrier, inc=1, device_id={"chan": chan_of(xy, (z + k) % 8)}, device_id_type=MESH)
        pl.semaphore_signal(barrier, inc=1, device_id={"chan": chan_of(other_xy(k), z)}, device_id_type=MESH)

    for k in (1, 3):
        pl.semaphore_signal(barrier, inc=1, device_id={"tm": (tm + k) % 4}, device_id_type=MESH)
    pl.semaphore_wait(barrier, 16)

    @pl.when(tm == 0)
    def _():
        frames[0:3] = jnp.zeros((3, INP, 2, ROOT, ROOT), BF)

    def relayout(i, carry):
        pltpu.make_async_copy(x_ref.at[i], xin.at[i], in_sem.at[i]).wait()
        for p in range(2):
            wide[p] = xin[i, p].astype(F32)
            for s in range(SPEC):
                frames[3 + s, i, p] = wide[p, pl.ds(s, ROOT, stride=SPEC), :].astype(BF)
        return carry

    lax.fori_loop(0, INP, relayout, 0)

    def halo(j):
        return pltpu.make_async_remote_copy(
            src_ref=frames.at[4 + j], dst_ref=frames.at[j],
            send_sem=halo_s.at[j], recv_sem=halo_r.at[j],
            device_id={"tm": (tm + 1) % 4}, device_id_type=MESH,
        )

    @pl.when(tm < 3)
    def _():
        for j in (2, 1, 0):
            halo(j).start()

    def spectrum(s):
        def pair(step, carry):
            sides = []
            for j in range(2):
                i = step * 2 + j
                parts = []
                for p in range(2):
                    total = taps_ref[0] * frames[s, i, p].astype(F32)
                    for k in range(1, TAPS):
                        total = total + taps_ref[k] * frames[s + k, i, p].astype(F32)
                    parts.append(total.astype(BF))
                sides.append(jnp.concatenate(parts, axis=0))
            both = jnp.concatenate(sides, axis=1)
            first = jnp.dot(m_ref[...], both, preferred_element_type=F32)
            rows = []
            for j in range(2):
                real = first[:ROOT, j * ROOT : (j + 1) * ROOT]
                imag = first[ROOT:, j * ROOT : (j + 1) * ROOT]
                cosine, sine = tw_ref[0], tw_ref[1]
                rows.append(
                    jnp.concatenate(
                        [(real * cosine + imag * sine).astype(BF), (imag * cosine - real * sine).astype(BF)],
                        axis=1,
                    )
                )
            second = lax.dot_general(
                m_ref[...], jnp.concatenate(rows, axis=0), (((1,), (1,)), ((), ())), preferred_element_type=F32
            )
            for j in range(2):
                turned[pl.ds(step * 2 + j, 2 * ROOT, stride=INP), :] = second[:, j * ROOT : (j + 1) * ROOT]
            return carry

        lax.fori_loop(0, INP // 2, pair, 0)

        def pack(g, carry):
            for p in range(2):
                for d in range(2):
                    row = pl.multiple_of((p * ROOT + 2 * g + d) * INP, INP)
                    lane = (p * 2 + d) * ROOT
                    snd[s, g % 8, g // 8, :, lane : lane + ROOT] = turned[pl.ds(row, INP), :].astype(BF)
            return carry

        lax.fori_loop(0, 64, pack, 0)

    def z_copy(s, k):
        to = (z + k) % 8
        return pltpu.make_async_remote_copy(
            src_ref=snd.at[s, to], dst_ref=mid.at[s, z],
            send_sem=z_s.at[s, k], recv_sem=z_r.at[s, k],
            device_id={"chan": chan_of(xy, to)}, device_id_type=MESH,
        )

    def xy_copy(s, k):
        to = other_xy(k)
        return pltpu.make_async_remote_copy(
            src_ref=mid.at[s, :, to], dst_ref=out_ref.at[s, xy],
            send_sem=xy_s.at[s, k], recv_sem=xy_r.at[s, k],
            device_id={"chan": chan_of(to, z)}, device_id_type=MESH,
        )

    def z_own(s):
        return pltpu.make_async_copy(snd.at[s, z], mid.at[s, z], loc_sem.at[s, 0])

    def xy_own(s):
        return pltpu.make_async_copy(mid.at[s, :, xy], out_ref.at[s, xy], loc_sem.at[s, 1])

    def send(s):
        for k in (4, 3, 5, 2, 6, 1, 7):
            z_copy(s, k).start()
        z_own(s).start()

    def forward(s):
        for k in range(1, 8):
            z_copy(s, k).wait_recv()
        z_own(s).wait()
        for k in range(1, 8):
            xy_copy(s, k).start()
        xy_own(s).start()

    def arrive(j):
        @pl.when(tm > 0)
        def _():
            halo(j).wait_recv()

    spectrum(3)
    send(3)
    arrive(2)
    spectrum(2)
    send(2)
    arrive(1)
    spectrum(1)
    send(1)
    forward(3)
    arrive(0)
    spectrum(0)
    send(0)
    forward(2)
    forward(1)
    forward(0)
    for s in range(SPEC):
        for k in range(1, 8):
            xy_copy(s, k).wait_recv()
        xy_own(s).wait()
    for s in range(SPEC):
        for k in range(1, 8):
            z_copy(s, k).wait_send()
            xy_copy(s, k).wait_send()

    @pl.when(tm < 3)
    def _():
        for j in range(3):
            halo(j).wait_send()


def turn(samples, taps):
    x = samples.reshape(INP, 2, SPEC, ROOT, ROOT).transpose(0, 1, 3, 2, 4).reshape(INP, 2, SPEC * ROOT, ROOT)
    vmem = pl.BlockSpec(memory_space=pltpu.VMEM)
    hbm = pl.BlockSpec(memory_space=pl.ANY)
    return pl.pallas_call(
        turn_kernel,
        out_shape=jax.ShapeDtypeStruct((SPEC, 8, 8, INP, 4 * ROOT), BF),
        in_specs=[hbm, vmem, vmem, vmem],
        out_specs=hbm,
        scratch_shapes=[
            pltpu.VMEM((INP, 2, SPEC * ROOT, ROOT), BF),
            pltpu.VMEM((2, SPEC * ROOT, ROOT), F32),
            pltpu.VMEM((7, INP, 2, ROOT, ROOT), BF),
            pltpu.VMEM((2 * ROOT * INP, ROOT), F32),
            pltpu.VMEM((SPEC, 8, 8, INP, 4 * ROOT), BF),
            pltpu.VMEM((SPEC, 8, 8, INP, 4 * ROOT), BF),
            pltpu.SemaphoreType.DMA((INP,)),
            pltpu.SemaphoreType.DMA((3,)),
            pltpu.SemaphoreType.DMA((3,)),
            pltpu.SemaphoreType.DMA((SPEC, 8)),
            pltpu.SemaphoreType.DMA((SPEC, 8)),
            pltpu.SemaphoreType.DMA((SPEC, 8)),
            pltpu.SemaphoreType.DMA((SPEC, 8)),
            pltpu.SemaphoreType.DMA((SPEC, 2)),
        ],
        compiler_params=pltpu.CompilerParams(
            collective_id=0, has_side_effects=True, vmem_limit_bytes=48 * 2**20
        ),
    )(x, taps.reshape(TAPS, ROOT, ROOT), jnp.asarray(dft_table(), BF), jnp.asarray(twiddle_table(), F32))


def corr_kernel(a_ref, out_ref, sib_snd, sib_rcv, x_snd, x_rcv, sib_s, sib_r, x_s, x_r):
    tm = lax.axis_index("tm")
    x_hi, core = tm // 2, tm % 2
    sibling = x_hi * 2 + 1 - core
    partner = (1 - x_hi) * 2 + core
    factor = 1.0 / 4096.0

    barrier = pltpu.get_barrier_semaphore()
    for other in (sibling, partner):
        pl.semaphore_signal(barrier, inc=1, device_id={"tm": other}, device_id_type=MESH)
    pl.semaphore_wait(barrier, 2)

    nt = (((1,), (1,)), ((), ()))

    def block(owner, j):
        rows = pl.ds(pl.multiple_of(owner * 256, 256), 256)
        cols = pl.ds(pl.multiple_of(j * 256, 256), 256)
        real = jnp.zeros((256, 256), F32)
        imag = jnp.zeros((256, 256), F32)
        for s in range(SPEC):
            left, right = a_ref[s, rows, :], a_ref[s, cols, :]
            real = real + lax.dot_general(left, right, nt, preferred_element_type=F32)
            imag = imag + lax.dot_general(left[:, 256:], right[:, :256], nt, preferred_element_type=F32)
            imag = imag - lax.dot_general(left[:, :256], right[:, 256:], nt, preferred_element_type=F32)
        return real * factor, imag * factor

    def sib_copy(h, j):
        return pltpu.make_async_remote_copy(
            src_ref=sib_snd.at[h, j], dst_ref=sib_rcv.at[h, j], send_sem=sib_s.at[h, j], recv_sem=sib_r.at[h, j],
            device_id={"tm": sibling}, device_id_type=MESH,
        )

    def x_copy(j):
        return pltpu.make_async_remote_copy(
            src_ref=x_snd.at[j], dst_ref=x_rcv.at[j], send_sem=x_s.at[j], recv_sem=x_r.at[j],
            device_id={"tm": partner}, device_id_type=MESH,
        )

    def far(j, carry):
        real, imag = block((1 - x_hi) * 2 + 1 - core, j)
        sib_snd[0, j, 0] = real.astype(BF)
        sib_snd[0, j, 1] = imag.astype(BF)
        sib_copy(0, j).start()
        real, imag = block((1 - x_hi) * 2 + core, j)
        sib_copy(0, j).wait_recv()
        x_snd[j, 0] = (real + sib_rcv[0, j, 0].astype(F32)).astype(BF)
        x_snd[j, 1] = (imag + sib_rcv[0, j, 1].astype(F32)).astype(BF)
        x_copy(j).start()
        return carry

    lax.fori_loop(0, 4, far, 0)

    def near(j, carry):
        real, imag = block(x_hi * 2 + 1 - core, j)
        sib_snd[1, j, 0] = real.astype(BF)
        sib_snd[1, j, 1] = imag.astype(BF)
        sib_copy(1, j).start()
        real, imag = block(x_hi * 2 + core, j)
        sib_copy(1, j).wait_recv()
        out_ref[:, pl.ds(pl.multiple_of(j * 256, 256), 256)] = real + sib_rcv[1, j, 0].astype(F32)
        out_ref[:, pl.ds(pl.multiple_of(j * 256 + 1024, 256), 256)] = imag + sib_rcv[1, j, 1].astype(F32)
        return carry

    lax.fori_loop(0, 4, near, 0)

    def finish(j, carry):
        x_copy(j).wait_recv()
        out_ref[:, pl.ds(pl.multiple_of(j * 256, 256), 256)] += x_rcv[j, 0].astype(F32)
        out_ref[:, pl.ds(pl.multiple_of(j * 256 + 1024, 256), 256)] += x_rcv[j, 1].astype(F32)
        return carry

    lax.fori_loop(0, 4, finish, 0)
    for j in range(4):
        sib_copy(0, j).wait_send()
        sib_copy(1, j).wait_send()
        x_copy(j).wait_send()


def corr(spectra):
    vmem = pl.BlockSpec(memory_space=pltpu.VMEM)
    return pl.pallas_call(
        corr_kernel,
        out_shape=jax.ShapeDtypeStruct((256, 2048), F32),
        in_specs=[vmem],
        out_specs=vmem,
        scratch_shapes=[
            pltpu.VMEM((2, 4, 2, 256, 256), BF),
            pltpu.VMEM((2, 4, 2, 256, 256), BF),
            pltpu.VMEM((4, 2, 256, 256), BF),
            pltpu.VMEM((4, 2, 256, 256), BF),
            pltpu.SemaphoreType.DMA((2, 4)),
            pltpu.SemaphoreType.DMA((2, 4)),
            pltpu.SemaphoreType.DMA((4,)),
            pltpu.SemaphoreType.DMA((4,)),
        ],
        compiler_params=pltpu.CompilerParams(
            collective_id=1, has_side_effects=True, vmem_limit_bytes=48 * 2**20
        ),
    )(spectra)


def body(samples, filter_taps):
    spectra = turn(samples, filter_taps).reshape(SPEC, 1024, 4 * ROOT)
    return corr(spectra)[None]


def solution(mesh):
    placed = (P("chan", None, "tm", None), P())
    return jax.shard_map(
        body, mesh=mesh, in_specs=placed, out_specs=P("chan", "tm", None), check_vma=False
    )
```

```python
import math

import jax
import jax.numpy as jnp
import numpy as np
from jax import lax
from jax.experimental import pallas as pl
from jax.experimental.pallas import tpu as pltpu
from jax.sharding import PartitionSpec as P

ROOT = 128
TAPS = 4
SPEC = 4
INP = 16
WIDE = 4 * ROOT
LATE = 7
Z_FIRST = (3, 2, 1)
MESH = pl.DeviceIdType.MESH
BF = jnp.bfloat16
F32 = jnp.float32
NT = (((1,), (1,)), ((), ()))


def dft_table():
    indices = np.arange(ROOT)
    angles = (indices[:, None] * indices[None, :] % ROOT) * (2.0 * math.pi / ROOT)
    cosine, sine = np.cos(angles), np.sin(angles)
    upper = np.concatenate([cosine, sine], axis=1)
    lower = np.concatenate([-sine, cosine], axis=1)
    return np.concatenate([upper, lower], axis=0)


def twiddle_table():
    indices = np.arange(ROOT)
    angles = (indices[:, None] * indices[None, :]) * (2.0 * math.pi / (ROOT * ROOT))
    return np.stack([np.cos(angles), np.sin(angles)]) / ROOT


def tables():
    quarters = dft_table().reshape(2, ROOT, 2, ROOT).transpose(0, 2, 1, 3).reshape(4, ROOT, ROOT)
    return np.concatenate([twiddle_table(), quarters]).astype(np.float32)


def kernel(
    x_ref, taps_ref, tab_ref, out_ref,
    xin, tin, taps, m, tw, wide, frames, turned, snd, mid, rcv, late,
    acc, mine, sib_snd, sib_rcv, x_snd, x_rcv,
    d1, d2, d1_snd, d1_rcv, d2_snd, d2_rcv, d1_xs, d1_xr, d2_xs, d2_xr,
    in_sem, const_sem, halo_s, halo_r, z_s, z_r, xy_s, xy_r, xl_s, xl_r, loc_sem,
    sib_s, sib_r, x_s, x_r, ds_s, ds_r, dx_s, dx_r,
):
    chan, tm = lax.axis_index("chan"), lax.axis_index("tm")
    x_lo, y, z = chan // 32, (chan // 8) % 4, chan % 8
    x_hi, core = tm // 2, tm % 2
    xy = x_lo * 4 + y
    sibling = x_hi * 2 + 1 - core
    partner = (1 - x_hi) * 2 + core

    def chan_of(xy_, z_):
        return xy_ * 8 + z_

    def other_xy(k):
        return ((x_lo + k // 4) % 2) * 4 + (y + k % 4) % 4

    constants = [
        pltpu.make_async_copy(taps_ref, tin, const_sem.at[0]),
        pltpu.make_async_copy(tab_ref, tw, const_sem.at[1]),
    ]
    for i in range(INP):
        pltpu.make_async_copy(x_ref.at[i], xin.at[i], in_sem.at[i]).start()
    for copy in constants:
        copy.start()

    barrier = pltpu.get_barrier_semaphore()
    for k in range(1, 8):
        pl.semaphore_signal(barrier, inc=1, device_id={"chan": chan_of(xy, (z + k) % 8)}, device_id_type=MESH)
        pl.semaphore_signal(barrier, inc=1, device_id={"chan": chan_of(other_xy(k), z)}, device_id_type=MESH)
    for k in range(1, 4):
        pl.semaphore_signal(barrier, inc=1, device_id={"tm": (tm + k) % 4}, device_id_type=MESH)

    @pl.when(tm == 0)
    def _():
        frames[0:3] = jnp.zeros((3, INP, 2, ROOT, ROOT), BF)

    for copy in constants:
        copy.wait()
    for k in range(TAPS):
        taps[k] = tin[pl.ds(k, ROOT, stride=TAPS), :]
        row, col = k // 2 * ROOT, k % 2 * ROOT
        m[row : row + ROOT, col : col + ROOT] = tw[2 + k].astype(BF)

    def relayout(i, carry):
        pltpu.make_async_copy(x_ref.at[i], xin.at[i], in_sem.at[i]).wait()
        for p in range(2):
            wide[p] = xin[i, p].astype(F32)
            for s in range(SPEC):
                frames[3 + s, i, p] = wide[p, pl.ds(s, ROOT, stride=SPEC), :].astype(BF)
        return carry

    lax.fori_loop(0, INP, relayout, 0)
    pl.semaphore_wait(barrier, 17)

    def halo(j):
        return pltpu.make_async_remote_copy(
            src_ref=frames.at[4 + j], dst_ref=frames.at[j],
            send_sem=halo_s.at[j], recv_sem=halo_r.at[j],
            device_id={"tm": (tm + 1) % 4}, device_id_type=MESH,
        )

    @pl.when(tm < 3)
    def _():
        for j in (2, 1, 0):
            halo(j).start()

    def spectrum(s):
        def pair(step, carry):
            sides = []
            for j in range(2):
                i = step * 2 + j
                parts = []
                for p in range(2):
                    total = taps[0] * frames[s, i, p].astype(F32)
                    for k in range(1, TAPS):
                        total = total + taps[k] * frames[s + k, i, p].astype(F32)
                    parts.append(total.astype(BF))
                sides.append(jnp.concatenate(parts, axis=0))
            both = jnp.concatenate(sides, axis=1)
            first = jnp.dot(m[...], both, preferred_element_type=F32)
            rows = []
            for j in range(2):
                real = first[:ROOT, j * ROOT : (j + 1) * ROOT]
                imag = first[ROOT:, j * ROOT : (j + 1) * ROOT]
                cosine, sine = tw[0], tw[1]
                rows.append(
                    jnp.concatenate(
                        [(real * cosine + imag * sine).astype(BF), (imag * cosine - real * sine).astype(BF)],
                        axis=1,
                    )
                )
            second = lax.dot_general(
                m[...], jnp.concatenate(rows, axis=0), NT, preferred_element_type=F32
            )
            for j in range(2):
                turned[pl.ds(step * 2 + j, 2 * ROOT, stride=INP), :] = second[:, j * ROOT : (j + 1) * ROOT]
            return carry

        lax.fori_loop(0, INP // 2, pair, 0)

        def pack(g, carry):
            for p in range(2):
                for d in range(2):
                    row = pl.multiple_of((p * ROOT + 2 * g + d) * INP, INP)
                    lane = (p * 2 + d) * ROOT
                    place = (g % 8, g // 8) if s in Z_FIRST else (g // 8, g % 8)
                    snd[s, place[0], place[1], :, lane : lane + ROOT] = turned[pl.ds(row, INP), :].astype(BF)
            return carry

        lax.fori_loop(0, 64, pack, 0)

    def remote(src, dst, send_sem, recv_sem, to_xy, to_z):
        return pltpu.make_async_remote_copy(
            src_ref=src, dst_ref=dst, send_sem=send_sem, recv_sem=recv_sem,
            device_id={"chan": chan_of(to_xy, to_z)}, device_id_type=MESH,
        )

    def z_copy(s, k):
        to, slot = (z + k) % 8, (11 - k) % 8
        if s in Z_FIRST and k != 4:
            src, dst = snd.at[s, to], mid.at[s, slot]
        elif k != 4:
            src, dst = mid.at[s, :, to], rcv.at[s, :, slot]
        elif s in Z_FIRST:
            src, dst = mid.at[s, LATE], late.at[s]
        else:
            src, dst = mid.at[s, :, to], late.at[s]
        return remote(src, dst, z_s.at[s, k], z_r.at[s, k], xy, to)

    def xy_copy(s, k):
        to = other_xy(k)
        if s in Z_FIRST:
            src, dst = mid.at[s, 0:LATE, to], rcv.at[s, xy, 0:LATE]
        else:
            src, dst = snd.at[s, to], mid.at[s, xy]
        return remote(src, dst, xy_s.at[s, k], xy_r.at[s, k], to, z)

    def xl_copy(s, k):
        to = other_xy(k)
        return remote(snd.at[s, (z + 4) % 8, to], mid.at[s, LATE, xy], xl_s.at[s, k], xl_r.at[s, k], to, z)

    def z_own(s):
        if s in Z_FIRST:
            return pltpu.make_async_copy(snd.at[s, z], mid.at[s, 3], loc_sem.at[s, 0])
        return pltpu.make_async_copy(mid.at[s, :, z], rcv.at[s, :, 3], loc_sem.at[s, 0])

    def xy_own(s):
        if s in Z_FIRST:
            return pltpu.make_async_copy(mid.at[s, 0:LATE, xy], rcv.at[s, xy, 0:LATE], loc_sem.at[s, 1])
        return pltpu.make_async_copy(snd.at[s, xy], mid.at[s, xy], loc_sem.at[s, 1])

    def xl_own(s):
        return pltpu.make_async_copy(snd.at[s, (z + 4) % 8, xy], mid.at[s, LATE, xy], loc_sem.at[s, 2])

    early = (3, 5, 2, 6, 1, 7)

    def send_z(s):
        for k in early:
            z_copy(s, k).start()
        z_own(s).start()

    def send_xy(s):
        for k in range(1, 8):
            xy_copy(s, k).start()
        xy_own(s).start()

    def send_xl(s):
        for k in range(1, 8):
            xl_copy(s, k).start()
        xl_own(s).start()

    def wait_z(s, some=early):
        for k in some:
            z_copy(s, k).wait_recv()

    def wait_xy(s):
        for k in range(1, 8):
            xy_copy(s, k).wait_recv()
        xy_own(s).wait()

    def wait_xl(s):
        for k in range(1, 8):
            xl_copy(s, k).wait_recv()
        xl_own(s).wait()

    def arrive(j):
        @pl.when(tm > 0)
        def _():
            halo(j).wait_recv()

    def rows_of(s, owner):
        return rcv[s, pl.ds(2 * owner, 2)].reshape(256, WIDE)

    def with_swapped(left):
        swapped = jnp.concatenate([left[:, 256:], -left[:, :256]], axis=1)
        return jnp.concatenate([left, swapped], axis=0)

    def product(s, owner, j):
        return lax.dot_general(with_swapped(rows_of(s, owner)), rows_of(s, j), NT, preferred_element_type=F32)

    def correlate(s, fresh):
        def step(n, carry):
            owner, j = n // 4, n % 4
            both = product(s, owner, j)
            if fresh:
                acc[owner, j] = both
            else:
                acc[owner, j] += both
            return carry

        lax.fori_loop(0, 16, step, 0)

    rcv[:, :, LATE] = jnp.zeros((SPEC, 8, INP, WIDE), BF)

    spectrum(3)
    send_z(3)
    arrive(2)
    spectrum(2)
    send_z(2)
    arrive(1)
    spectrum(1)
    wait_z(3)
    z_own(3).wait()
    send_xy(3)
    send_z(1)
    arrive(0)
    spectrum(0)
    send_xy(0)
    wait_z(2)
    z_own(2).wait()
    send_xy(2)
    wait_xy(0)
    send_z(0)
    for s in (3, 2, 1):
        send_xl(s)
    wait_xy(3)
    correlate(3, True)
    wait_z(1)
    z_own(1).wait()
    send_xy(1)
    wait_xy(2)
    correlate(2, False)
    for s in (3, 2, 1):
        wait_xl(s)
    wait_xy(1)
    correlate(1, False)
    wait_z(0, early[4:])
    for s in (3, 2, 1, 0):
        z_copy(s, 4).start()
    wait_z(0, early[:4])
    z_own(0).wait()

    factor = 1.0 / 4096.0

    def sib_copy(h, j):
        return pltpu.make_async_remote_copy(
            src_ref=sib_snd.at[h, j], dst_ref=sib_rcv.at[h, j], send_sem=sib_s.at[h, j], recv_sem=sib_r.at[h, j],
            device_id={"tm": sibling}, device_id_type=MESH,
        )

    def x_copy(j):
        return pltpu.make_async_remote_copy(
            src_ref=x_snd.at[j, :, 0:112], dst_ref=x_rcv.at[j, :, 0:112], send_sem=x_s.at[j], recv_sem=x_r.at[j],
            device_id={"tm": partner}, device_id_type=MESH,
        )

    def block(owner, j):
        return (acc[owner, j] + product(0, owner, j)) * factor

    def far(j, carry):
        sib_snd[0, j] = block((1 - x_hi) * 2 + 1 - core, j).astype(BF)
        sib_copy(0, j).start()
        both = block((1 - x_hi) * 2 + core, j)
        sib_copy(0, j).wait_recv()
        x_snd[j] = (both + sib_rcv[0, j].astype(F32)).astype(BF).reshape(4, 128, 256)
        x_copy(j).start()
        return carry

    lax.fori_loop(0, 4, far, 0)

    def near(j, carry):
        sib_snd[1, j] = block(x_hi * 2 + 1 - core, j).astype(BF)
        sib_copy(1, j).start()
        both = block(x_hi * 2 + core, j)
        sib_copy(1, j).wait_recv()
        mine[j] = both + sib_rcv[1, j].astype(F32)
        return carry

    lax.fori_loop(0, 4, near, 0)

    def late_part(s, fresh):
        z_copy(s, 4).wait_recv()
        rcv[s, :, LATE] = late[s]
        tail = late[s].reshape(128, WIDE)
        tail_both = with_swapped(tail)

        def step(o, carry):
            right = rows_of(s, o)
            column = lax.dot_general(with_swapped(right), tail, NT, preferred_element_type=F32)
            row = lax.dot_general(tail_both, right, NT, preferred_element_type=F32)
            if fresh:
                d1[o] = column
                d2[o] = row
            else:
                d1[o] += column
                d2[o] += row
            return carry

        lax.fori_loop(0, 4, step, 0)

    late_part(3, True)
    late_part(2, False)
    late_part(1, False)
    late_part(0, False)

    def d_rows(owner):
        re = d2[:, pl.ds(pl.multiple_of(owner * 32, 32), 32), :]
        im = d2[:, pl.ds(pl.multiple_of(owner * 32 + 128, 32), 32), :]
        return re * factor, im * factor

    def ds_copies(h):
        return [
            pltpu.make_async_remote_copy(
                src_ref=d1_snd.at[h], dst_ref=d1_rcv.at[h], send_sem=ds_s.at[h, 0], recv_sem=ds_r.at[h, 0],
                device_id={"tm": sibling}, device_id_type=MESH,
            ),
            pltpu.make_async_remote_copy(
                src_ref=d2_snd.at[h], dst_ref=d2_rcv.at[h], send_sem=ds_s.at[h, 1], recv_sem=ds_r.at[h, 1],
                device_id={"tm": sibling}, device_id_type=MESH,
            ),
        ]

    dx_copies = [
        pltpu.make_async_remote_copy(
            src_ref=d1_xs, dst_ref=d1_xr, send_sem=dx_s.at[0], recv_sem=dx_r.at[0],
            device_id={"tm": partner}, device_id_type=MESH,
        ),
        pltpu.make_async_remote_copy(
            src_ref=d2_xs, dst_ref=d2_xr, send_sem=dx_s.at[1], recv_sem=dx_r.at[1],
            device_id={"tm": partner}, device_id_type=MESH,
        ),
    ]

    for h, owner in ((0, (1 - x_hi) * 2 + 1 - core), (1, x_hi * 2 + 1 - core)):
        d1_snd[h] = (d1[owner] * factor).astype(BF)
        re, im = d_rows(owner)
        d2_snd[h, 0] = re.astype(BF)
        d2_snd[h, 1] = im.astype(BF)
        for copy in ds_copies(h):
            copy.start()
    owner = (1 - x_hi) * 2 + core
    for copy in ds_copies(0):
        copy.wait_recv()
    d1_xs[...] = (d1[owner] * factor + d1_rcv[0].astype(F32)).astype(BF)
    re, im = d_rows(owner)
    d2_xs[0] = (re + d2_rcv[0, 0].astype(F32)).astype(BF)
    d2_xs[1] = (im + d2_rcv[0, 1].astype(F32)).astype(BF)
    for copy in dx_copies:
        copy.start()

    for j in range(4):
        x_copy(j).wait_recv()
    for copy in ds_copies(1):
        copy.wait_recv()
    for copy in dx_copies:
        copy.wait_recv()

    owner = x_hi * 2 + core
    turn = (z + 5) % 8
    lanes = lax.broadcasted_iota(jnp.int32, (256, ROOT), 1)
    columns = [
        d1[owner, pl.ds(part * 256, 256)] * factor
        + d1_rcv[1, pl.ds(part * 256, 256)].astype(F32)
        + d1_xr[pl.ds(part * 256, 256)].astype(F32)
        for part in range(2)
    ]
    own_rows = d_rows(owner)
    for part in range(2):
        rows = own_rows[part] + d2_rcv[1, part].astype(F32) + d2_xr[part].astype(F32)
        for c in range(8):
            j, half = c // 2, (c % 2) * ROOT
            tile = mine[j, part * 256 : part * 256 + 256, half : half + ROOT] + x_rcv[
                j, part * 2 : part * 2 + 2, :, half : half + ROOT
            ].reshape(256, ROOT).astype(F32)
            moved = columns[part] if c == 7 else pltpu.roll(columns[part], 112 - 16 * c, 1)
            tile = jnp.where(lanes >= 112, moved, tile)
            pieces = []
            for v in range(2):
                pieces.append(tile[v * 128 : v * 128 + 112])
                pieces.append(rows[j, v * 16 : v * 16 + 16, half : half + ROOT])
            tile = pltpu.roll(jnp.concatenate(pieces, axis=0), turn * 16, 1)
            for v in range(2):
                for t in range(8):
                    to = pl.multiple_of(v * 128 + ((turn + t) % 8) * 16, 16)
                    at = part * 1024 + c * ROOT
                    out_ref[pl.ds(to, 16), at : at + ROOT] = tile[v * 128 + t * 16 : v * 128 + t * 16 + 16]

    for s in range(SPEC):
        for k in range(1, 8):
            z_copy(s, k).wait_send()
            xy_copy(s, k).wait_send()
    for s in Z_FIRST:
        for k in range(1, 8):
            xl_copy(s, k).wait_send()
    for j in range(4):
        sib_copy(0, j).wait_send()
        sib_copy(1, j).wait_send()
        x_copy(j).wait_send()
    for h in range(2):
        for copy in ds_copies(h):
            copy.wait_send()
    for copy in dx_copies:
        copy.wait_send()

    @pl.when(tm < 3)
    def _():
        for j in range(3):
            halo(j).wait_send()


def body(samples, filter_taps):
    x = samples.reshape(INP, 2, SPEC, ROOT, ROOT).transpose(0, 1, 3, 2, 4).reshape(INP, 2, SPEC * ROOT, ROOT)
    t = filter_taps.reshape(TAPS, ROOT, ROOT).transpose(1, 0, 2).reshape(TAPS * ROOT, ROOT)
    vmem = pl.BlockSpec(memory_space=pltpu.VMEM)
    hbm = pl.BlockSpec(memory_space=pl.ANY)
    dma = pltpu.SemaphoreType.DMA
    out = pl.pallas_call(
        kernel,
        out_shape=jax.ShapeDtypeStruct((256, 2048), F32),
        in_specs=[hbm, hbm, hbm],
        out_specs=vmem,
        scratch_shapes=[
            pltpu.VMEM((INP, 2, SPEC * ROOT, ROOT), BF),
            pltpu.VMEM((TAPS * ROOT, ROOT), F32),
            pltpu.VMEM((TAPS, ROOT, ROOT), F32),
            pltpu.VMEM((2 * ROOT, 2 * ROOT), BF),
            pltpu.VMEM((6, ROOT, ROOT), F32),
            pltpu.VMEM((2, SPEC * ROOT, ROOT), F32),
            pltpu.VMEM((7, INP, 2, ROOT, ROOT), BF),
            pltpu.VMEM((2 * ROOT * INP, ROOT), F32),
            pltpu.VMEM((SPEC, 8, 8, INP, WIDE), BF),
            pltpu.VMEM((SPEC, 8, 8, INP, WIDE), BF),
            pltpu.VMEM((SPEC, 8, 8, INP, WIDE), BF),
            pltpu.VMEM((SPEC, 8, INP, WIDE), BF),
            pltpu.VMEM((4, 4, 512, 256), F32),
            pltpu.VMEM((4, 512, 256), F32),
            pltpu.VMEM((2, 4, 512, 256), BF),
            pltpu.VMEM((2, 4, 512, 256), BF),
            pltpu.VMEM((4, 4, 128, 256), BF),
            pltpu.VMEM((4, 4, 128, 256), BF),
            pltpu.VMEM((4, 512, 128), F32),
            pltpu.VMEM((4, 256, 256), F32),
            pltpu.VMEM((2, 512, 128), BF),
            pltpu.VMEM((2, 512, 128), BF),
            pltpu.VMEM((2, 2, 4, 32, 256), BF),
            pltpu.VMEM((2, 2, 4, 32, 256), BF),
            pltpu.VMEM((512, 128), BF),
            pltpu.VMEM((512, 128), BF),
            pltpu.VMEM((2, 4, 32, 256), BF),
            pltpu.VMEM((2, 4, 32, 256), BF),
            dma((INP,)), dma((3,)), dma((3,)), dma((3,)),
            dma((SPEC, 8)), dma((SPEC, 8)),
            dma((SPEC, 8)), dma((SPEC, 8)),
            dma((SPEC, 8)), dma((SPEC, 8)),
            dma((SPEC, 3)),
            dma((2, 4)), dma((2, 4)), dma((4,)), dma((4,)),
            dma((2, 2)), dma((2, 2)), dma((2,)), dma((2,)),
        ],
        compiler_params=pltpu.CompilerParams(
            collective_id=0, has_side_effects=True, vmem_limit_bytes=48 * 2**20
        ),
    )(x, t, jnp.asarray(tables()))
    return out[None]


def solution(mesh):
    placed = (P("chan", None, "tm", None), P())
    return jax.shard_map(
        body, mesh=mesh, in_specs=placed, out_specs=P("chan", "tm", None), check_vma=False
    )
```

```python
import math

import jax
import jax.numpy as jnp
import numpy as np
from jax import lax
from jax.experimental import pallas as pl
from jax.experimental.pallas import tpu as pltpu
from jax.sharding import PartitionSpec as P

ROOT = 128
TAPS = 4
SPEC = 4
INP = 16
GROUP = 4
HOP = 4
WIDE = 4 * ROOT
LATE = 7
ROWS = LATE * 2 * INP
Z_FIRST = (3, 2, 1)
MESH = pl.DeviceIdType.MESH
BF = jnp.bfloat16
F32 = jnp.float32
NT = (((1,), (1,)), ((), ()))


def dft_table():
    indices = np.arange(ROOT)
    angles = (indices[:, None] * indices[None, :] % ROOT) * (2.0 * math.pi / ROOT)
    cosine, sine = np.cos(angles), np.sin(angles)
    upper = np.concatenate([cosine, sine], axis=1)
    lower = np.concatenate([-sine, cosine], axis=1)
    return np.concatenate([upper, lower], axis=0)


def twiddle_table():
    indices = np.arange(ROOT)
    angles = (indices[:, None] * indices[None, :]) * (2.0 * math.pi / (ROOT * ROOT))
    return np.stack([np.cos(angles), np.sin(angles)]) / ROOT


def tables():
    quarters = dft_table().reshape(2, ROOT, 2, ROOT).transpose(0, 2, 1, 3).reshape(4, ROOT, ROOT)
    return np.concatenate([twiddle_table(), quarters]).astype(np.float32).reshape(6 * ROOT, ROOT)


def kernel(
    x_ref, tab_ref, out_ref,
    xin, tin, taps, m, wide, frames, hop, turned, snd, mid, rcv,
    acc, acc3, left, mine, sib_snd, sib3_snd, sib_rcv, sib3_rcv, x_snd, x3_snd, x_rcv, x3_rcv,
    d1, d2, d1_snd, d1_rcv, d2_snd, d2_rcv, d1_xs, d1_xr, d2_xs, d2_xr,
    in_sem, const_sem, halo_s, halo_r, hop_s, hop_r, newest_s, newest_r, z_s, z_r, xy_s, xy_r, xl_s, xl_r, loc_sem,
    sib_s, sib_r, x_s, x_r, ds_s, ds_r, dx_s, dx_r,
):
    chan, tm = lax.axis_index("chan"), lax.axis_index("tm")
    x_lo, y, z = chan // 32, (chan // 8) % 4, chan % 8
    x_hi, core = tm // 2, tm % 2
    xy = x_lo * 4 + y
    sibling = x_hi * 2 + 1 - core
    partner = (1 - x_hi) * 2 + core

    def chan_of(xy_, z_):
        return xy_ * 8 + z_

    def other_xy(k):
        return ((x_lo + k // 4) % 2) * 4 + (y + k % 4) % 4

    constants = pltpu.make_async_copy(tab_ref, tin, const_sem.at[0])
    constants.start()
    for i in range(INP):
        pltpu.make_async_copy(x_ref.at[i], xin.at[i], in_sem.at[i]).start()

    barrier = pltpu.get_barrier_semaphore()
    for k in range(1, 8):
        pl.semaphore_signal(barrier, inc=1, device_id={"chan": chan_of(xy, (z + k) % 8)}, device_id_type=MESH)
        pl.semaphore_signal(barrier, inc=1, device_id={"chan": chan_of(other_xy(k), z)}, device_id_type=MESH)
    for k in range(1, 4):
        pl.semaphore_signal(barrier, inc=1, device_id={"tm": (tm + k) % 4}, device_id_type=MESH)
    pl.semaphore_signal(
        barrier, inc=1, device_id={"chan": chan_of(other_xy(4), z), "tm": (tm + 3) % 4}, device_id_type=MESH
    )

    @pl.when(tm == 0)
    def _():
        frames[0:3] = jnp.zeros((3, INP, 2, ROOT, ROOT), BF)

    constants.wait()
    for k in range(4):
        taps[k] = tin[pl.ds(k, ROOT, stride=TAPS), :]
        row, col = k // 2 * ROOT, k % 2 * ROOT
        m[row : row + ROOT, col : col + ROOT] = tin[(6 + k) * ROOT : (7 + k) * ROOT].astype(BF)

    pl.semaphore_wait(barrier, 18)

    def halo(j, rest):
        inputs = slice(INP - HOP, INP) if rest else slice(0, INP - HOP)
        return pltpu.make_async_remote_copy(
            src_ref=frames.at[4 + j, inputs], dst_ref=frames.at[j, inputs],
            send_sem=halo_s.at[rest, j], recv_sem=halo_r.at[rest, j],
            device_id={"tm": (tm + 1) % 4}, device_id_type=MESH,
        )

    def hop_out(j):
        return pltpu.make_async_remote_copy(
            src_ref=frames.at[4 + j, INP - HOP : INP], dst_ref=hop.at[j],
            send_sem=halo_s.at[1, j], recv_sem=hop_r.at[j],
            device_id={"chan": chan_of(other_xy(4), z), "tm": (tm + 1) % 4}, device_id_type=MESH,
        )

    def hop_on(j):
        return pltpu.make_async_remote_copy(
            src_ref=hop.at[j], dst_ref=frames.at[j, INP - HOP : INP],
            send_sem=hop_s.at[j], recv_sem=halo_r.at[1, j],
            device_id={"chan": chan_of(other_xy(4), z)}, device_id_type=MESH,
        )

    def newest(step):
        inputs = pl.ds(step * GROUP, GROUP)
        return pltpu.make_async_remote_copy(
            src_ref=frames.at[6, inputs], dst_ref=frames.at[2, inputs],
            send_sem=newest_s.at[step], recv_sem=newest_r.at[step],
            device_id={"tm": (tm + 1) % 4}, device_id_type=MESH,
        )

    def transform(start, sides):
        for a in range(0, GROUP, 2):
            first = jnp.dot(m[...], jnp.concatenate(sides[a : a + 2], axis=1), preferred_element_type=F32)
            rows = []
            for j in range(2):
                real = first[:ROOT, j * ROOT : (j + 1) * ROOT]
                imag = first[ROOT:, j * ROOT : (j + 1) * ROOT]
                cosine, sine = tin[4 * ROOT : 5 * ROOT], tin[5 * ROOT : 6 * ROOT]
                rows.append(
                    jnp.concatenate(
                        [(real * cosine + imag * sine).astype(BF), (imag * cosine - real * sine).astype(BF)],
                        axis=1,
                    )
                )
            second = lax.dot_general(
                m[...], jnp.concatenate(rows, axis=0), NT, preferred_element_type=F32
            )
            for j in range(2):
                turned[pl.ds(start + a + j, 2 * ROOT, stride=INP), :] = second[:, j * ROOT : (j + 1) * ROOT]

    def pack(s):
        def step(g, carry):
            for v in range(8):
                for p in range(2):
                    for d in range(2):
                        row = pl.multiple_of((p * ROOT + 2 * (g * 8 + v) + d) * INP, INP)
                        lane = (p * 2 + d) * ROOT
                        place = (v, g) if s in Z_FIRST else (g, v)
                        snd[s, place[0], place[1], :, lane : lane + ROOT] = turned[pl.ds(row, INP), :].astype(BF)
            return carry

        lax.fori_loop(0, 8, step, 0)

    def first_spectrum():
        def group(step, carry):
            sides = []
            for j in range(GROUP):
                i = step * GROUP + j
                pltpu.make_async_copy(x_ref.at[i], xin.at[i], in_sem.at[i]).wait()
                parts = []
                for p in range(2):
                    wide[2 * j + p] = xin[i, p].astype(F32)
                    total = None
                    for k in range(TAPS):
                        frame = wide[2 * j + p, pl.ds(k, ROOT, stride=SPEC), :]
                        frames[3 + k, i, p] = frame.astype(BF)
                        total = taps[k] * frame if k == 0 else total + taps[k] * frame
                    parts.append(total.astype(BF))
                sides.append(jnp.concatenate(parts, axis=0))

            @pl.when(tm < 3)
            def _():
                newest(step).start()

            transform(step * GROUP, sides)
            return carry

        lax.fori_loop(0, INP // GROUP, group, 0)

        @pl.when(tm == 1)
        def _():
            hop_out(1).start()
            hop_out(0).start()

        @pl.when((tm == 0) | (tm == 2))
        def _():
            halo(1, 1).start()
            halo(0, 1).start()

        @pl.when(tm < 3)
        def _():
            halo(1, 0).start()
            halo(0, 0).start()

        pack(3)

    def spectrum(s):
        def group(step, carry):
            sides = []
            for j in range(GROUP):
                i = step * GROUP + j
                parts = []
                for p in range(2):
                    total = taps[0] * frames[s, i, p].astype(F32)
                    for k in range(1, TAPS):
                        total = total + taps[k] * frames[s + k, i, p].astype(F32)
                    parts.append(total.astype(BF))
                sides.append(jnp.concatenate(parts, axis=0))
            transform(step * GROUP, sides)
            return carry

        lax.fori_loop(0, INP // GROUP, group, 0)
        pack(s)

    def remote(src, dst, send_sem, recv_sem, to_xy, to_z):
        return pltpu.make_async_remote_copy(
            src_ref=src, dst_ref=dst, send_sem=send_sem, recv_sem=recv_sem,
            device_id={"chan": chan_of(to_xy, to_z)}, device_id_type=MESH,
        )

    def z_copy(s, k):
        to, slot = (z + k) % 8, (11 - k) % 8
        if s in Z_FIRST and k != 4:
            src, dst = snd.at[s, to], mid.at[s, slot]
        elif k != 4:
            src, dst = mid.at[s, :, to], rcv.at[s, slot]
        elif s in Z_FIRST:
            src, dst = mid.at[s, LATE], rcv.at[s, LATE]
        else:
            src, dst = mid.at[s, :, to], rcv.at[s, LATE]
        return remote(src, dst, z_s.at[s, k], z_r.at[s, k], xy, to)

    def xy_copy(s, k):
        to = other_xy(k)
        if s in Z_FIRST:
            src, dst = mid.at[s, 0:LATE, to], rcv.at[s, 0:LATE, xy]
        else:
            src, dst = snd.at[s, to], mid.at[s, xy]
        return remote(src, dst, xy_s.at[s, k], xy_r.at[s, k], to, z)

    def xl_copy(s, k):
        to = other_xy(k)
        return remote(snd.at[s, (z + 4) % 8, to], mid.at[s, LATE, xy], xl_s.at[s, k], xl_r.at[s, k], to, z)

    def z_own(s):
        if s in Z_FIRST:
            return pltpu.make_async_copy(snd.at[s, z], mid.at[s, 3], loc_sem.at[s, 0])
        return pltpu.make_async_copy(mid.at[s, :, z], rcv.at[s, 3], loc_sem.at[s, 0])

    def xy_own(s):
        if s in Z_FIRST:
            return pltpu.make_async_copy(mid.at[s, 0:LATE, xy], rcv.at[s, 0:LATE, xy], loc_sem.at[s, 1])
        return pltpu.make_async_copy(snd.at[s, xy], mid.at[s, xy], loc_sem.at[s, 1])

    def xl_own(s):
        return pltpu.make_async_copy(snd.at[s, (z + 4) % 8, xy], mid.at[s, LATE, xy], loc_sem.at[s, 2])

    early = (3, 5, 2, 6, 1, 7)

    def send_z(s):
        for k in early:
            z_copy(s, k).start()
        z_own(s).start()

    def send_xy(s):
        for k in range(1, 8):
            xy_copy(s, k).start()
        xy_own(s).start()

    def send_xl(s):
        for k in range(1, 8):
            xl_copy(s, k).start()
        xl_own(s).start()

    def wait_z(s, some=early):
        for k in some:
            z_copy(s, k).wait_recv()

    def wait_xy(s):
        for k in range(1, 8):
            xy_copy(s, k).wait_recv()
        xy_own(s).wait()

    def wait_xl(s):
        for k in range(1, 8):
            xl_copy(s, k).wait_recv()
        xl_own(s).wait()

    def pass_on():
        @pl.when(tm == 2)
        def _():
            for j in (1, 0):
                hop_out(j).wait_recv()
                hop_on(j).start()

    def arrive(j):
        @pl.when(tm > 0)
        def _():
            if j == 2:
                for step in range(INP // GROUP):
                    newest(step).wait_recv()
            else:
                halo(j, 0).wait_recv()
                halo(j, 1).wait_recv()

    def rows_of(s, owner):
        return rcv[s, 0:LATE, pl.ds(2 * owner, 2)].reshape(ROWS, WIDE)

    def columns_of(s, j):
        if j == 3:
            return rcv[s, 6].reshape(ROOT, WIDE)
        return rcv[s, 2 * j : 2 * j + 2].reshape(256, WIDE)

    def with_swapped(left):
        swapped = jnp.concatenate([left[:, 256:], -left[:, :256]], axis=1)
        return jnp.concatenate([left, swapped], axis=0)

    def times(left, right):
        return lax.dot_general(left, right, NT, preferred_element_type=F32)

    def piece(refs, j):
        return refs[1] if j == 3 else refs[0].at[j]

    def acc_of(owner, j):
        return acc3.at[owner] if j == 3 else acc.at[owner, j]

    def correlate(s, fresh):
        def step(owner, carry):
            left = with_swapped(rows_of(s, owner))
            for j in range(4):
                both = times(left, columns_of(s, j))
                if fresh:
                    acc_of(owner, j)[...] = both
                else:
                    acc_of(owner, j)[...] += both
            return carry

        lax.fori_loop(0, 4, step, 0)

    first_spectrum()
    send_z(3)
    arrive(2)
    mine[LATE] = jnp.zeros((512, ROOT), F32)
    spectrum(2)
    send_z(2)
    pass_on()
    arrive(1)
    spectrum(1)
    wait_z(3)
    z_own(3).wait()
    send_xy(3)
    send_z(1)
    arrive(0)
    spectrum(0)
    send_xy(0)
    wait_z(2)
    z_own(2).wait()
    send_xy(2)
    wait_xy(0)
    send_z(0)
    for s in (3, 2, 1):
        send_xl(s)
    wait_xy(3)
    correlate(3, True)
    wait_z(1)
    z_own(1).wait()
    send_xy(1)
    wait_xy(2)
    correlate(2, False)
    for s in (3, 2, 1):
        wait_xl(s)
    wait_xy(1)
    wait_z(0, early[4:])
    for s in (3, 2, 1, 0):
        z_copy(s, 4).start()
    wait_z(0, early[:4])
    z_own(0).wait()

    factor = 1.0 / 4096.0

    def part_of(refs, h, j):
        return refs[1].at[h] if j == 3 else refs[0].at[h, j]

    def sib_copy(h, j):
        return pltpu.make_async_remote_copy(
            src_ref=part_of((sib_snd, sib3_snd), h, j), dst_ref=part_of((sib_rcv, sib3_rcv), h, j),
            send_sem=sib_s.at[h, j], recv_sem=sib_r.at[h, j],
            device_id={"tm": sibling}, device_id_type=MESH,
        )

    def x_copy(j):
        return pltpu.make_async_remote_copy(
            src_ref=piece((x_snd, x3_snd), j), dst_ref=piece((x_rcv, x3_rcv), j),
            send_sem=x_s.at[j], recv_sem=x_r.at[j],
            device_id={"tm": partner}, device_id_type=MESH,
        )

    def block(owner, side, j):
        last = times(left[side, 0], columns_of(0, j)) + times(left[side, 1], columns_of(1, j))
        return (acc_of(owner, j)[...] + last) * factor

    def store_mine(j, both):
        for part in range(2):
            rows = both[part * ROWS : part * ROWS + ROWS]
            mine[2 * j, part * 256 : part * 256 + ROWS] = rows[:, :ROOT]
            if j < 3:
                mine[2 * j + 1, part * 256 : part * 256 + ROWS] = rows[:, ROOT:]

    for h, hi in ((0, 1 - x_hi), (1, x_hi)):
        given, kept = hi * 2 + 1 - core, hi * 2 + core
        for s in range(2):
            left[0, s] = with_swapped(rows_of(s, given))
            left[1, s] = with_swapped(rows_of(s, kept))

        def give(j):
            both = block(given, 0, j)
            part_of((sib_snd, sib3_snd), h, j)[...] = both.astype(BF)
            sib_copy(h, j).start()

        def keep(j):
            both = block(kept, 1, j)
            sib_copy(h, j).wait_recv()
            both = both + part_of((sib_rcv, sib3_rcv), h, j)[...].astype(F32)
            if h == 0:
                piece((x_snd, x3_snd), j)[...] = both.astype(BF)
                x_copy(j).start()
            else:
                store_mine(j, both)

        give(0)
        give(1)
        keep(0)
        give(2)
        keep(1)
        give(3)
        keep(2)
        keep(3)

    def late_part(s, fresh):
        z_copy(s, 4).wait_recv()
        tail = rcv[s, LATE].reshape(ROOT, WIDE)
        tail_both = with_swapped(tail)

        def column(o, carry):
            both = times(with_swapped(rows_of(s, o)), tail)
            if fresh:
                d1[o] = both
            else:
                d1[o] += both
            return carry

        lax.fori_loop(0, 4, column, 0)

        def row(j, carry):
            both = times(tail_both, rcv[s, pl.ds(2 * j, 2)].reshape(256, WIDE))
            if fresh:
                d2[j] = both
            else:
                d2[j] += both
            return carry

        lax.fori_loop(0, 4, row, 0)

    late_part(3, True)
    late_part(2, False)
    late_part(1, False)
    late_part(0, False)

    def d_rows(owner):
        re = d2[:, pl.ds(pl.multiple_of(owner * 32, 32), 32), :]
        im = d2[:, pl.ds(pl.multiple_of(owner * 32 + 128, 32), 32), :]
        return re * factor, im * factor

    def ds_copies(h):
        return [
            pltpu.make_async_remote_copy(
                src_ref=d1_snd.at[h], dst_ref=d1_rcv.at[h], send_sem=ds_s.at[h, 0], recv_sem=ds_r.at[h, 0],
                device_id={"tm": sibling}, device_id_type=MESH,
            ),
            pltpu.make_async_remote_copy(
                src_ref=d2_snd.at[h], dst_ref=d2_rcv.at[h], send_sem=ds_s.at[h, 1], recv_sem=ds_r.at[h, 1],
                device_id={"tm": sibling}, device_id_type=MESH,
            ),
        ]

    dx_copies = [
        pltpu.make_async_remote_copy(
            src_ref=d1_xs, dst_ref=d1_xr, send_sem=dx_s.at[0], recv_sem=dx_r.at[0],
            device_id={"tm": partner}, device_id_type=MESH,
        ),
        pltpu.make_async_remote_copy(
            src_ref=d2_xs, dst_ref=d2_xr, send_sem=dx_s.at[1], recv_sem=dx_r.at[1],
            device_id={"tm": partner}, device_id_type=MESH,
        ),
    ]

    for h, owner in ((0, (1 - x_hi) * 2 + 1 - core), (1, x_hi * 2 + 1 - core)):
        d1_snd[h] = (d1[owner] * factor).astype(BF)
        re, im = d_rows(owner)
        d2_snd[h, 0] = re.astype(BF)
        d2_snd[h, 1] = im.astype(BF)
        for copy in ds_copies(h):
            copy.start()
    owner = (1 - x_hi) * 2 + core
    for copy in ds_copies(0):
        copy.wait_recv()
    d1_xs[...] = (d1[owner] * factor + d1_rcv[0].astype(F32)).astype(BF)
    re, im = d_rows(owner)
    d2_xs[0] = (re + d2_rcv[0, 0].astype(F32)).astype(BF)
    d2_xs[1] = (im + d2_rcv[0, 1].astype(F32)).astype(BF)
    for copy in dx_copies:
        copy.start()

    turn = (z + 5) % 8
    block_of = lax.broadcasted_iota(jnp.int32, (32, ROOT), 1) // INP

    def transposed(tiles):
        for bit in (1, 2, 4):
            low = block_of // bit % 2 == 0
            swapped = list(tiles)
            for a in range(8):
                if a & bit == 0:
                    one, two = tiles[a], tiles[a | bit]
                    swapped[a] = jnp.where(low, one, pltpu.roll(two, bit * INP, 1))
                    swapped[a | bit] = jnp.where(low, pltpu.roll(one, ROOT - bit * INP, 1), two)
            tiles = swapped
        return tiles

    for j in range(4):
        x_copy(j).wait_recv()
        for part in range(2):
            rows = piece((x_rcv, x3_rcv), j)[part * ROWS : part * ROWS + ROWS].astype(F32)
            mine[2 * j, part * 256 : part * 256 + ROWS] += rows[:, :ROOT]
            if j < 3:
                mine[2 * j + 1, part * 256 : part * 256 + ROWS] += rows[:, ROOT:]

    def place(part, t):
        at = pl.ds(pl.multiple_of(part * 256 + t * 32, 32), 32)
        tiles = transposed([mine[(g + 8 - turn) % 8, at, :] for g in range(8)])
        for v in range(2):
            to = pl.ds(pl.multiple_of(v * ROOT + (turn + t) % 8 * INP, INP), INP)
            for c in range(8):
                out_ref[to, part * 1024 + c * ROOT : part * 1024 + c * ROOT + ROOT] = tiles[c][v * INP : v * INP + INP]

    def place_early(t, carry):
        for part in range(2):
            place(part, t)
        return carry

    lax.fori_loop(0, LATE, place_early, 0)

    owner = x_hi * 2 + core
    for copy in ds_copies(1):
        copy.wait_recv()
    own_rows = d_rows(owner)
    for copy in dx_copies:
        copy.wait_recv()

    last = (z + 4) % 8

    def place_columns(t, carry):
        for part in range(2):
            at = pl.ds(pl.multiple_of(part * ROWS + t * 32, 32), 32)
            both = d1[owner, at] * factor + d1_rcv[1, at].astype(F32) + d1_xr[at].astype(F32)
            both = pltpu.roll(both, last * INP, 1)
            for c in range(8):
                moved = both if c == 0 else pltpu.roll(both, ROOT - c * INP, 1)
                cols = slice(part * 1024 + c * ROOT, part * 1024 + c * ROOT + ROOT)
                for v in range(2):
                    to = pl.ds(pl.multiple_of(v * ROOT + (turn + t) % 8 * INP, INP), INP)
                    out_ref[to, cols] = jnp.where(
                        block_of[:INP] == last, moved[v * INP : v * INP + INP], out_ref[to, cols]
                    )
        return carry

    lax.fori_loop(0, LATE, place_columns, 0)

    for part in range(2):
        rows = own_rows[part] + d2_rcv[1, part].astype(F32) + d2_xr[part].astype(F32)
        for t in range(8):
            mine[t, part * 256 + ROWS : part * 256 + 256] = rows[t // 2, :, t % 2 * ROOT : t % 2 * ROOT + ROOT]
        place(part, LATE)

    for s in range(SPEC):
        for k in range(1, 8):
            z_copy(s, k).wait_send()
            xy_copy(s, k).wait_send()
    for s in Z_FIRST:
        for k in range(1, 8):
            xl_copy(s, k).wait_send()
    for j in range(4):
        sib_copy(0, j).wait_send()
        sib_copy(1, j).wait_send()
        x_copy(j).wait_send()
    for h in range(2):
        for copy in ds_copies(h):
            copy.wait_send()
    for copy in dx_copies:
        copy.wait_send()

    @pl.when(tm < 3)
    def _():
        for j in range(2):
            halo(j, 0).wait_send()
            halo(j, 1).wait_send()
        for step in range(INP // GROUP):
            newest(step).wait_send()

    @pl.when(tm == 2)
    def _():
        for j in range(2):
            hop_on(j).wait_send()


def body(samples, filter_taps):
    x = samples.reshape(INP, 2, SPEC, ROOT, ROOT).transpose(0, 1, 3, 2, 4).reshape(INP, 2, SPEC * ROOT, ROOT)
    t = filter_taps.reshape(TAPS, ROOT, ROOT).transpose(1, 0, 2).reshape(TAPS * ROOT, ROOT)
    vmem = pl.BlockSpec(memory_space=pltpu.VMEM)
    hbm = pl.BlockSpec(memory_space=pl.ANY)
    dma = pltpu.SemaphoreType.DMA
    out = pl.pallas_call(
        kernel,
        out_shape=jax.ShapeDtypeStruct((256, 2048), F32),
        in_specs=[hbm, hbm],
        out_specs=vmem,
        scratch_shapes=[
            pltpu.VMEM((INP, 2, SPEC * ROOT, ROOT), BF),
            pltpu.VMEM((10 * ROOT, ROOT), F32),
            pltpu.VMEM((TAPS, ROOT, ROOT), F32),
            pltpu.VMEM((2 * ROOT, 2 * ROOT), BF),
            pltpu.VMEM((2 * GROUP, SPEC * ROOT, ROOT), F32),
            pltpu.VMEM((7, INP, 2, ROOT, ROOT), BF),
            pltpu.VMEM((2, HOP, 2, ROOT, ROOT), BF),
            pltpu.VMEM((2 * ROOT * INP, ROOT), F32),
            pltpu.VMEM((SPEC, 8, 8, INP, WIDE), BF),
            pltpu.VMEM((SPEC, 8, 8, INP, WIDE), BF),
            pltpu.VMEM((SPEC, 8, 8, INP, WIDE), BF),
            pltpu.VMEM((4, 3, 2 * ROWS, 256), F32),
            pltpu.VMEM((4, 2 * ROWS, ROOT), F32),
            pltpu.VMEM((2, 2, 2 * ROWS, WIDE), BF),
            pltpu.VMEM((8, 512, ROOT), F32),
            pltpu.VMEM((2, 3, 2 * ROWS, 256), BF),
            pltpu.VMEM((2, 2 * ROWS, ROOT), BF),
            pltpu.VMEM((2, 3, 2 * ROWS, 256), BF),
            pltpu.VMEM((2, 2 * ROWS, ROOT), BF),
            pltpu.VMEM((3, 2 * ROWS, 256), BF),
            pltpu.VMEM((2 * ROWS, ROOT), BF),
            pltpu.VMEM((3, 2 * ROWS, 256), BF),
            pltpu.VMEM((2 * ROWS, ROOT), BF),
            pltpu.VMEM((4, 2 * ROWS, ROOT), F32),
            pltpu.VMEM((4, 256, 256), F32),
            pltpu.VMEM((2, 2 * ROWS, ROOT), BF),
            pltpu.VMEM((2, 2 * ROWS, ROOT), BF),
            pltpu.VMEM((2, 2, 4, 32, 256), BF),
            pltpu.VMEM((2, 2, 4, 32, 256), BF),
            pltpu.VMEM((2 * ROWS, ROOT), BF),
            pltpu.VMEM((2 * ROWS, ROOT), BF),
            pltpu.VMEM((2, 4, 32, 256), BF),
            pltpu.VMEM((2, 4, 32, 256), BF),
            dma((INP,)), dma((1,)), dma((2, 2)), dma((2, 2)), dma((2,)), dma((2,)),
            dma((INP // GROUP,)), dma((INP // GROUP,)),
            dma((SPEC, 8)), dma((SPEC, 8)),
            dma((SPEC, 8)), dma((SPEC, 8)),
            dma((SPEC, 8)), dma((SPEC, 8)),
            dma((SPEC, 3)),
            dma((2, 4)), dma((2, 4)), dma((4,)), dma((4,)),
            dma((2, 2)), dma((2, 2)), dma((2,)), dma((2,)),
        ],
        compiler_params=pltpu.CompilerParams(
            collective_id=0, has_side_effects=True, vmem_limit_bytes=50 * 2**20
        ),
    )(x, jnp.concatenate([t, jnp.asarray(tables())]))
    return out[None]


def solution(mesh):
    placed = (P("chan", None, "tm", None), P())
    return jax.shard_map(
        body, mesh=mesh, in_specs=placed, out_specs=P("chan", "tm", None), check_vma=False
    )
```

```python
import math

import jax
import jax.numpy as jnp
import numpy as np
from jax import lax
from jax.experimental import pallas as pl
from jax.experimental.pallas import tpu as pltpu
from jax.sharding import PartitionSpec as P

ROOT = 128
TAPS = 4
SPEC = 4
INP = 16
GROUP = 4
HOP = 2
WIDE = 4 * ROOT
LATE = 7
ROWS = LATE * 2 * INP
Z_FIRST = (3, 2, 1)
MESH = pl.DeviceIdType.MESH
BF = jnp.bfloat16
F32 = jnp.float32
NT = (((1,), (1,)), ((), ()))


def dft_table():
    indices = np.arange(ROOT)
    angles = (indices[:, None] * indices[None, :] % ROOT) * (2.0 * math.pi / ROOT)
    cosine, sine = np.cos(angles), np.sin(angles)
    upper = np.concatenate([cosine, sine], axis=1)
    lower = np.concatenate([-sine, cosine], axis=1)
    return np.concatenate([upper, lower], axis=0)


def twiddle_table():
    indices = np.arange(ROOT)
    angles = (indices[:, None] * indices[None, :]) * (2.0 * math.pi / (ROOT * ROOT))
    return np.stack([np.cos(angles), np.sin(angles)]) / ROOT


def tables():
    quarters = dft_table().reshape(2, ROOT, 2, ROOT).transpose(0, 2, 1, 3).reshape(4, ROOT, ROOT)
    return np.concatenate([twiddle_table(), quarters]).astype(np.float32).reshape(6 * ROOT, ROOT)


def kernel(
    x_ref, tab_ref, out_ref,
    xin, tin, taps, m, wide, frames, hop, turned, snd, mid, rcv,
    acc, acc3, left, mine, sib_snd, sib3_snd, sib_rcv, sib3_rcv, x_snd, x3_snd, x_rcv, x3_rcv,
    d1, d2, d1_snd, d1_rcv, d2_snd, d2_rcv, d1_xs, d1_xr, d2_xs, d2_xr,
    in_sem, const_sem, halo_s, halo_r, hop_s, hop_r, newest_s, newest_r, z_s, z_r, xy_s, xy_r, xl_s, xl_r, loc_sem,
    sib_s, sib_r, x_s, x_r, ds_s, ds_r, dx_s, dx_r,
):
    chan, tm = lax.axis_index("chan"), lax.axis_index("tm")
    x_lo, y, z = chan // 32, (chan // 8) % 4, chan % 8
    x_hi, core = tm // 2, tm % 2
    xy = x_lo * 4 + y
    sibling = x_hi * 2 + 1 - core
    partner = (1 - x_hi) * 2 + core

    def chan_of(xy_, z_):
        return xy_ * 8 + z_

    def other_xy(k):
        return ((x_lo + k // 4) % 2) * 4 + (y + k % 4) % 4

    constants = pltpu.make_async_copy(tab_ref, tin, const_sem.at[0])
    constants.start()
    for i in range(INP):
        pltpu.make_async_copy(x_ref.at[i], xin.at[i], in_sem.at[i]).start()

    barrier = pltpu.get_barrier_semaphore()
    for k in range(1, 8):
        pl.semaphore_signal(barrier, inc=1, device_id={"chan": chan_of(xy, (z + k) % 8)}, device_id_type=MESH)
        pl.semaphore_signal(barrier, inc=1, device_id={"chan": chan_of(other_xy(k), z)}, device_id_type=MESH)
    for k in range(1, 4):
        pl.semaphore_signal(barrier, inc=1, device_id={"tm": (tm + k) % 4}, device_id_type=MESH)
    pl.semaphore_signal(
        barrier, inc=1, device_id={"chan": chan_of(other_xy(4), z), "tm": (tm + 3) % 4}, device_id_type=MESH
    )

    @pl.when(tm == 0)
    def _():
        frames[0:3] = jnp.zeros((3, INP, 2, ROOT, ROOT), BF)

    constants.wait()
    for k in range(4):
        taps[k] = tin[pl.ds(k, ROOT, stride=TAPS), :]
        row, col = k // 2 * ROOT, k % 2 * ROOT
        m[row : row + ROOT, col : col + ROOT] = tin[(6 + k) * ROOT : (7 + k) * ROOT].astype(BF)

    pl.semaphore_wait(barrier, 18)

    def halo(j, rest):
        inputs = slice(INP - HOP, INP) if rest else slice(0, INP - HOP)
        return pltpu.make_async_remote_copy(
            src_ref=frames.at[4 + j, inputs], dst_ref=frames.at[j, inputs],
            send_sem=halo_s.at[rest, j], recv_sem=halo_r.at[rest, j],
            device_id={"tm": (tm + 1) % 4}, device_id_type=MESH,
        )

    def hop_out(j):
        return pltpu.make_async_remote_copy(
            src_ref=frames.at[4 + j, INP - HOP : INP], dst_ref=hop.at[j],
            send_sem=halo_s.at[1, j], recv_sem=hop_r.at[j],
            device_id={"chan": chan_of(other_xy(4), z), "tm": (tm + 1) % 4}, device_id_type=MESH,
        )

    def hop_on(j):
        return pltpu.make_async_remote_copy(
            src_ref=hop.at[j], dst_ref=frames.at[j, INP - HOP : INP],
            send_sem=hop_s.at[j], recv_sem=halo_r.at[1, j],
            device_id={"chan": chan_of(other_xy(4), z)}, device_id_type=MESH,
        )

    def newest(step):
        inputs = pl.ds(step * GROUP, GROUP)
        return pltpu.make_async_remote_copy(
            src_ref=frames.at[6, inputs], dst_ref=frames.at[2, inputs],
            send_sem=newest_s.at[step], recv_sem=newest_r.at[step],
            device_id={"tm": (tm + 1) % 4}, device_id_type=MESH,
        )

    def transform(start, sides):
        for a in range(0, GROUP, 2):
            first = jnp.dot(m[...], jnp.concatenate(sides[a : a + 2], axis=1), preferred_element_type=F32)
            rows = []
            for j in range(2):
                real = first[:ROOT, j * ROOT : (j + 1) * ROOT]
                imag = first[ROOT:, j * ROOT : (j + 1) * ROOT]
                cosine, sine = tin[4 * ROOT : 5 * ROOT], tin[5 * ROOT : 6 * ROOT]
                rows.append(
                    jnp.concatenate(
                        [(real * cosine + imag * sine).astype(BF), (imag * cosine - real * sine).astype(BF)],
                        axis=1,
                    )
                )
            second = lax.dot_general(
                m[...], jnp.concatenate(rows, axis=0), NT, preferred_element_type=F32
            )
            for j in range(2):
                turned[pl.ds(start + a + j, 2 * ROOT, stride=INP), :] = second[:, j * ROOT : (j + 1) * ROOT]

    def pack(s):
        def step(g, carry):
            for v in range(8):
                for p in range(2):
                    for d in range(2):
                        row = pl.multiple_of((p * ROOT + 2 * (g * 8 + v) + d) * INP, INP)
                        lane = (p * 2 + d) * ROOT
                        place = (v, g) if s in Z_FIRST else (g, v)
                        snd[s, place[0], place[1], :, lane : lane + ROOT] = turned[pl.ds(row, INP), :].astype(BF)
            return carry

        lax.fori_loop(0, 8, step, 0)

    def first_spectrum():
        def group(step, carry):
            sides = []
            for j in range(GROUP):
                i = step * GROUP + j
                pltpu.make_async_copy(x_ref.at[i], xin.at[i], in_sem.at[i]).wait()
                parts = []
                for p in range(2):
                    wide[2 * j + p] = xin[i, p].astype(F32)
                    total = None
                    for k in range(TAPS):
                        frame = wide[2 * j + p, pl.ds(k, ROOT, stride=SPEC), :]
                        frames[3 + k, i, p] = frame.astype(BF)
                        total = taps[k] * frame if k == 0 else total + taps[k] * frame
                    parts.append(total.astype(BF))
                sides.append(jnp.concatenate(parts, axis=0))

            @pl.when(tm < 3)
            def _():
                newest(step).start()

            transform(step * GROUP, sides)
            return carry

        lax.fori_loop(0, INP // GROUP, group, 0)

        @pl.when(tm == 1)
        def _():
            hop_out(1).start()
            hop_out(0).start()

        @pl.when((tm == 0) | (tm == 2))
        def _():
            halo(1, 1).start()
            halo(0, 1).start()

        @pl.when(tm < 3)
        def _():
            halo(1, 0).start()
            halo(0, 0).start()

        pack(3)

    def spectrum(s):
        def group(step, carry):
            sides = []
            for j in range(GROUP):
                i = step * GROUP + j
                parts = []
                for p in range(2):
                    total = taps[0] * frames[s, i, p].astype(F32)
                    for k in range(1, TAPS):
                        total = total + taps[k] * frames[s + k, i, p].astype(F32)
                    parts.append(total.astype(BF))
                sides.append(jnp.concatenate(parts, axis=0))
            transform(step * GROUP, sides)
            return carry

        lax.fori_loop(0, INP // GROUP, group, 0)
        pack(s)

    def remote(src, dst, send_sem, recv_sem, to_xy, to_z):
        return pltpu.make_async_remote_copy(
            src_ref=src, dst_ref=dst, send_sem=send_sem, recv_sem=recv_sem,
            device_id={"chan": chan_of(to_xy, to_z)}, device_id_type=MESH,
        )

    def z_copy(s, k):
        to, slot = (z + k) % 8, (11 - k) % 8
        if s in Z_FIRST and k != 4:
            src, dst = snd.at[s, to], mid.at[s, slot]
        elif k != 4:
            src, dst = mid.at[s, :, to], rcv.at[s, slot]
        elif s in Z_FIRST:
            src, dst = mid.at[s, LATE], rcv.at[s, LATE]
        else:
            src, dst = mid.at[s, :, to], rcv.at[s, LATE]
        return remote(src, dst, z_s.at[s, k], z_r.at[s, k], xy, to)

    def xy_copy(s, k):
        to = other_xy(k)
        if s in Z_FIRST:
            src, dst = mid.at[s, 0:LATE, to], rcv.at[s, 0:LATE, xy]
        else:
            src, dst = snd.at[s, to], mid.at[s, xy]
        return remote(src, dst, xy_s.at[s, k], xy_r.at[s, k], to, z)

    def xl_copy(s, k):
        to = other_xy(k)
        return remote(snd.at[s, (z + 4) % 8, to], mid.at[s, LATE, xy], xl_s.at[s, k], xl_r.at[s, k], to, z)

    def z_own(s):
        if s in Z_FIRST:
            return pltpu.make_async_copy(snd.at[s, z], mid.at[s, 3], loc_sem.at[s, 0])
        return pltpu.make_async_copy(mid.at[s, :, z], rcv.at[s, 3], loc_sem.at[s, 0])

    def xy_own(s):
        if s in Z_FIRST:
            return pltpu.make_async_copy(mid.at[s, 0:LATE, xy], rcv.at[s, 0:LATE, xy], loc_sem.at[s, 1])
        return pltpu.make_async_copy(snd.at[s, xy], mid.at[s, xy], loc_sem.at[s, 1])

    def xl_own(s):
        return pltpu.make_async_copy(snd.at[s, (z + 4) % 8, xy], mid.at[s, LATE, xy], loc_sem.at[s, 2])

    early = (3, 5, 2, 6, 1, 7)

    def send_z(s):
        for k in early:
            z_copy(s, k).start()
        z_own(s).start()

    def send_xy(s):
        for k in (5, 7, 6, 4, 2, 1, 3):
            xy_copy(s, k).start()
        xy_own(s).start()

    def send_xl(s):
        for k in range(1, 8):
            xl_copy(s, k).start()
        xl_own(s).start()

    def wait_z(s, some=early):
        for k in some:
            z_copy(s, k).wait_recv()

    def wait_xy(s):
        for k in range(1, 8):
            xy_copy(s, k).wait_recv()
        xy_own(s).wait()

    def wait_xl(s):
        for k in range(1, 8):
            xl_copy(s, k).wait_recv()
        xl_own(s).wait()

    def pass_on():
        @pl.when(tm == 2)
        def _():
            for j in (1, 0):
                hop_out(j).wait_recv()
                hop_on(j).start()

    def arrive(j):
        @pl.when(tm > 0)
        def _():
            if j == 2:
                for step in range(INP // GROUP):
                    newest(step).wait_recv()
            else:
                halo(j, 0).wait_recv()
                halo(j, 1).wait_recv()

    def rows_of(s, owner):
        return rcv[s, 0:LATE, pl.ds(2 * owner, 2)].reshape(ROWS, WIDE)

    def columns_of(s, j):
        if j == 3:
            return rcv[s, 6].reshape(ROOT, WIDE)
        return rcv[s, 2 * j : 2 * j + 2].reshape(256, WIDE)

    def with_swapped(left):
        swapped = jnp.concatenate([left[:, 256:], -left[:, :256]], axis=1)
        return jnp.concatenate([left, swapped], axis=0)

    def times(left, right):
        return lax.dot_general(left, right, NT, preferred_element_type=F32)

    def piece(refs, j):
        return refs[1] if j == 3 else refs[0].at[j]

    def acc_of(owner, j):
        return acc3.at[owner] if j == 3 else acc.at[owner, j]

    def correlate(s, fresh):
        def step(owner, carry):
            left = with_swapped(rows_of(s, owner))
            for j in range(4):
                both = times(left, columns_of(s, j))
                if fresh:
                    acc_of(owner, j)[...] = both
                else:
                    acc_of(owner, j)[...] += both
            return carry

        lax.fori_loop(0, 4, step, 0)

    first_spectrum()
    send_z(3)
    arrive(2)
    mine[LATE] = jnp.zeros((512, ROOT), F32)
    spectrum(2)
    send_z(2)
    pass_on()
    arrive(1)
    spectrum(1)
    wait_z(3)
    z_own(3).wait()
    send_xy(3)
    send_z(1)
    arrive(0)
    spectrum(0)
    send_xy(0)
    wait_z(2)
    z_own(2).wait()
    send_xy(2)
    wait_xy(0)
    send_z(0)
    for s in (3, 2, 1):
        send_xl(s)
    wait_xy(3)
    correlate(3, True)
    wait_z(1)
    z_own(1).wait()
    send_xy(1)
    wait_xy(2)
    correlate(2, False)
    for s in (3, 2, 1):
        wait_xl(s)
    wait_xy(1)
    wait_z(0, early[4:])
    for s in (3, 2, 1, 0):
        z_copy(s, 4).start()
    wait_z(0, early[:4])
    z_own(0).wait()

    factor = 1.0 / 4096.0

    def part_of(refs, h, j):
        return refs[1].at[h] if j == 3 else refs[0].at[h, j]

    def sib_copy(h, j):
        return pltpu.make_async_remote_copy(
            src_ref=part_of((sib_snd, sib3_snd), h, j), dst_ref=part_of((sib_rcv, sib3_rcv), h, j),
            send_sem=sib_s.at[h, j], recv_sem=sib_r.at[h, j],
            device_id={"tm": sibling}, device_id_type=MESH,
        )

    def x_copy(j):
        return pltpu.make_async_remote_copy(
            src_ref=piece((x_snd, x3_snd), j), dst_ref=piece((x_rcv, x3_rcv), j),
            send_sem=x_s.at[j], recv_sem=x_r.at[j],
            device_id={"tm": partner}, device_id_type=MESH,
        )

    def block(owner, side, j):
        last = times(left[side, 0], columns_of(0, j)) + times(left[side, 1], columns_of(1, j))
        return (acc_of(owner, j)[...] + last) * factor

    def store_mine(j, both):
        for part in range(2):
            rows = both[part * ROWS : part * ROWS + ROWS]
            mine[2 * j, part * 256 : part * 256 + ROWS] = rows[:, :ROOT]
            if j < 3:
                mine[2 * j + 1, part * 256 : part * 256 + ROWS] = rows[:, ROOT:]

    for h, hi in ((0, 1 - x_hi), (1, x_hi)):
        given, kept = hi * 2 + 1 - core, hi * 2 + core
        for s in range(2):
            left[0, s] = with_swapped(rows_of(s, given))
            left[1, s] = with_swapped(rows_of(s, kept))

        def give(j):
            both = block(given, 0, j)
            part_of((sib_snd, sib3_snd), h, j)[...] = both.astype(BF)
            sib_copy(h, j).start()

        def keep(j):
            both = block(kept, 1, j)
            sib_copy(h, j).wait_recv()
            both = both + part_of((sib_rcv, sib3_rcv), h, j)[...].astype(F32)
            if h == 0:
                piece((x_snd, x3_snd), j)[...] = both.astype(BF)
                x_copy(j).start()
            else:
                store_mine(j, both)

        give(0)
        give(1)
        keep(0)
        give(2)
        keep(1)
        give(3)
        keep(2)
        keep(3)

    def late_part(s, fresh):
        z_copy(s, 4).wait_recv()
        tail = rcv[s, LATE].reshape(ROOT, WIDE)
        tail_both = with_swapped(tail)

        def column(o, carry):
            both = times(with_swapped(rows_of(s, o)), tail)
            if fresh:
                d1[o] = both
            else:
                d1[o] += both
            return carry

        lax.fori_loop(0, 4, column, 0)

        def row(j, carry):
            both = times(tail_both, rcv[s, pl.ds(2 * j, 2)].reshape(256, WIDE))
            if fresh:
                d2[j] = both
            else:
                d2[j] += both
            return carry

        lax.fori_loop(0, 4, row, 0)

    late_part(3, True)
    late_part(2, False)
    late_part(1, False)
    late_part(0, False)

    def d_rows(owner):
        re = d2[:, pl.ds(pl.multiple_of(owner * 32, 32), 32), :]
        im = d2[:, pl.ds(pl.multiple_of(owner * 32 + 128, 32), 32), :]
        return re * factor, im * factor

    def ds_copies(h):
        return [
            pltpu.make_async_remote_copy(
                src_ref=d1_snd.at[h], dst_ref=d1_rcv.at[h], send_sem=ds_s.at[h, 0], recv_sem=ds_r.at[h, 0],
                device_id={"tm": sibling}, device_id_type=MESH,
            ),
            pltpu.make_async_remote_copy(
                src_ref=d2_snd.at[h], dst_ref=d2_rcv.at[h], send_sem=ds_s.at[h, 1], recv_sem=ds_r.at[h, 1],
                device_id={"tm": sibling}, device_id_type=MESH,
            ),
        ]

    dx_copies = [
        pltpu.make_async_remote_copy(
            src_ref=d1_xs, dst_ref=d1_xr, send_sem=dx_s.at[0], recv_sem=dx_r.at[0],
            device_id={"tm": partner}, device_id_type=MESH,
        ),
        pltpu.make_async_remote_copy(
            src_ref=d2_xs, dst_ref=d2_xr, send_sem=dx_s.at[1], recv_sem=dx_r.at[1],
            device_id={"tm": partner}, device_id_type=MESH,
        ),
    ]

    for h, owner in ((0, (1 - x_hi) * 2 + 1 - core), (1, x_hi * 2 + 1 - core)):
        d1_snd[h] = (d1[owner] * factor).astype(BF)
        re, im = d_rows(owner)
        d2_snd[h, 0] = re.astype(BF)
        d2_snd[h, 1] = im.astype(BF)
        for copy in ds_copies(h):
            copy.start()
    owner = (1 - x_hi) * 2 + core
    for copy in ds_copies(0):
        copy.wait_recv()
    d1_xs[...] = (d1[owner] * factor + d1_rcv[0].astype(F32)).astype(BF)
    re, im = d_rows(owner)
    d2_xs[0] = (re + d2_rcv[0, 0].astype(F32)).astype(BF)
    d2_xs[1] = (im + d2_rcv[0, 1].astype(F32)).astype(BF)
    for copy in dx_copies:
        copy.start()

    turn = (z + 5) % 8
    block_of = lax.broadcasted_iota(jnp.int32, (32, ROOT), 1) // INP

    def transposed(tiles):
        for bit in (1, 2, 4):
            low = block_of // bit % 2 == 0
            swapped = list(tiles)
            for a in range(8):
                if a & bit == 0:
                    one, two = tiles[a], tiles[a | bit]
                    swapped[a] = jnp.where(low, one, pltpu.roll(two, bit * INP, 1))
                    swapped[a | bit] = jnp.where(low, pltpu.roll(one, ROOT - bit * INP, 1), two)
            tiles = swapped
        return tiles

    for j in range(4):
        x_copy(j).wait_recv()
        for part in range(2):
            rows = piece((x_rcv, x3_rcv), j)[part * ROWS : part * ROWS + ROWS].astype(F32)
            mine[2 * j, part * 256 : part * 256 + ROWS] += rows[:, :ROOT]
            if j < 3:
                mine[2 * j + 1, part * 256 : part * 256 + ROWS] += rows[:, ROOT:]

    def place(part, t):
        at = pl.ds(pl.multiple_of(part * 256 + t * 32, 32), 32)
        tiles = transposed([mine[(g + 8 - turn) % 8, at, :] for g in range(8)])
        for v in range(2):
            to = pl.ds(pl.multiple_of(v * ROOT + (turn + t) % 8 * INP, INP), INP)
            for c in range(8):
                out_ref[to, part * 1024 + c * ROOT : part * 1024 + c * ROOT + ROOT] = tiles[c][v * INP : v * INP + INP]

    def place_early(t, carry):
        for part in range(2):
            place(part, t)
        return carry

    lax.fori_loop(0, LATE, place_early, 0)

    owner = x_hi * 2 + core
    for copy in ds_copies(1):
        copy.wait_recv()
    own_rows = d_rows(owner)
    for copy in dx_copies:
        copy.wait_recv()

    last = (z + 4) % 8

    def place_columns(t, carry):
        for part in range(2):
            at = pl.ds(pl.multiple_of(part * ROWS + t * 32, 32), 32)
            both = d1[owner, at] * factor + d1_rcv[1, at].astype(F32) + d1_xr[at].astype(F32)
            both = pltpu.roll(both, last * INP, 1)
            for c in range(8):
                moved = both if c == 0 else pltpu.roll(both, ROOT - c * INP, 1)
                cols = slice(part * 1024 + c * ROOT, part * 1024 + c * ROOT + ROOT)
                for v in range(2):
                    to = pl.ds(pl.multiple_of(v * ROOT + (turn + t) % 8 * INP, INP), INP)
                    out_ref[to, cols] = jnp.where(
                        block_of[:INP] == last, moved[v * INP : v * INP + INP], out_ref[to, cols]
                    )
        return carry

    lax.fori_loop(0, LATE, place_columns, 0)

    for part in range(2):
        rows = own_rows[part] + d2_rcv[1, part].astype(F32) + d2_xr[part].astype(F32)
        for t in range(8):
            mine[t, part * 256 + ROWS : part * 256 + 256] = rows[t // 2, :, t % 2 * ROOT : t % 2 * ROOT + ROOT]
        place(part, LATE)

    for s in range(SPEC):
        for k in range(1, 8):
            z_copy(s, k).wait_send()
            xy_copy(s, k).wait_send()
    for s in Z_FIRST:
        for k in range(1, 8):
            xl_copy(s, k).wait_send()
    for j in range(4):
        sib_copy(0, j).wait_send()
        sib_copy(1, j).wait_send()
        x_copy(j).wait_send()
    for h in range(2):
        for copy in ds_copies(h):
            copy.wait_send()
    for copy in dx_copies:
        copy.wait_send()

    @pl.when(tm < 3)
    def _():
        for j in range(2):
            halo(j, 0).wait_send()
            halo(j, 1).wait_send()
        for step in range(INP // GROUP):
            newest(step).wait_send()

    @pl.when(tm == 2)
    def _():
        for j in range(2):
            hop_on(j).wait_send()


def body(samples, filter_taps):
    x = samples.reshape(INP, 2, SPEC, ROOT, ROOT).transpose(0, 1, 3, 2, 4).reshape(INP, 2, SPEC * ROOT, ROOT)
    t = filter_taps.reshape(TAPS, ROOT, ROOT).transpose(1, 0, 2).reshape(TAPS * ROOT, ROOT)
    vmem = pl.BlockSpec(memory_space=pltpu.VMEM)
    hbm = pl.BlockSpec(memory_space=pl.ANY)
    dma = pltpu.SemaphoreType.DMA
    out = pl.pallas_call(
        kernel,
        out_shape=jax.ShapeDtypeStruct((256, 2048), F32),
        in_specs=[hbm, hbm],
        out_specs=vmem,
        scratch_shapes=[
            pltpu.VMEM((INP, 2, SPEC * ROOT, ROOT), BF),
            pltpu.VMEM((10 * ROOT, ROOT), F32),
            pltpu.VMEM((TAPS, ROOT, ROOT), F32),
            pltpu.VMEM((2 * ROOT, 2 * ROOT), BF),
            pltpu.VMEM((2 * GROUP, SPEC * ROOT, ROOT), F32),
            pltpu.VMEM((7, INP, 2, ROOT, ROOT), BF),
            pltpu.VMEM((2, HOP, 2, ROOT, ROOT), BF),
            pltpu.VMEM((2 * ROOT * INP, ROOT), F32),
            pltpu.VMEM((SPEC, 8, 8, INP, WIDE), BF),
            pltpu.VMEM((SPEC, 8, 8, INP, WIDE), BF),
            pltpu.VMEM((SPEC, 8, 8, INP, WIDE), BF),
            pltpu.VMEM((4, 3, 2 * ROWS, 256), F32),
            pltpu.VMEM((4, 2 * ROWS, ROOT), F32),
            pltpu.VMEM((2, 2, 2 * ROWS, WIDE), BF),
            pltpu.VMEM((8, 512, ROOT), F32),
            pltpu.VMEM((2, 3, 2 * ROWS, 256), BF),
            pltpu.VMEM((2, 2 * ROWS, ROOT), BF),
            pltpu.VMEM((2, 3, 2 * ROWS, 256), BF),
            pltpu.VMEM((2, 2 * ROWS, ROOT), BF),
            pltpu.VMEM((3, 2 * ROWS, 256), BF),
            pltpu.VMEM((2 * ROWS, ROOT), BF),
            pltpu.VMEM((3, 2 * ROWS, 256), BF),
            pltpu.VMEM((2 * ROWS, ROOT), BF),
            pltpu.VMEM((4, 2 * ROWS, ROOT), F32),
            pltpu.VMEM((4, 256, 256), F32),
            pltpu.VMEM((2, 2 * ROWS, ROOT), BF),
            pltpu.VMEM((2, 2 * ROWS, ROOT), BF),
            pltpu.VMEM((2, 2, 4, 32, 256), BF),
            pltpu.VMEM((2, 2, 4, 32, 256), BF),
            pltpu.VMEM((2 * ROWS, ROOT), BF),
            pltpu.VMEM((2 * ROWS, ROOT), BF),
            pltpu.VMEM((2, 4, 32, 256), BF),
            pltpu.VMEM((2, 4, 32, 256), BF),
            dma((INP,)), dma((1,)), dma((2, 2)), dma((2, 2)), dma((2,)), dma((2,)),
            dma((INP // GROUP,)), dma((INP // GROUP,)),
            dma((SPEC, 8)), dma((SPEC, 8)),
            dma((SPEC, 8)), dma((SPEC, 8)),
            dma((SPEC, 8)), dma((SPEC, 8)),
            dma((SPEC, 3)),
            dma((2, 4)), dma((2, 4)), dma((4,)), dma((4,)),
            dma((2, 2)), dma((2, 2)), dma((2,)), dma((2,)),
        ],
        compiler_params=pltpu.CompilerParams(
            collective_id=0, has_side_effects=True, vmem_limit_bytes=50 * 2**20
        ),
    )(x, jnp.concatenate([t, jnp.asarray(tables())]))
    return out[None]


def solution(mesh):
    placed = (P("chan", None, "tm", None), P())
    return jax.shard_map(
        body, mesh=mesh, in_specs=placed, out_specs=P("chan", "tm", None), check_vma=False
    )
```

```python
import math

import jax
import jax.numpy as jnp
import numpy as np
from jax import lax
from jax.experimental import pallas as pl
from jax.experimental.pallas import tpu as pltpu
from jax.sharding import PartitionSpec as P

ROOT = 128
TAPS = 4
SPEC = 4
INP = 16
GROUP = 4
HOP = 2
WIDE = 4 * ROOT
LATE = 7
ROWS = LATE * 2 * INP
Z_FIRST = (3, 2, 1)
MESH = pl.DeviceIdType.MESH
BF = jnp.bfloat16
F32 = jnp.float32
NT = (((1,), (1,)), ((), ()))


def dft_table():
    indices = np.arange(ROOT)
    angles = (indices[:, None] * indices[None, :] % ROOT) * (2.0 * math.pi / ROOT)
    cosine, sine = np.cos(angles), np.sin(angles)
    upper = np.concatenate([cosine, sine], axis=1)
    lower = np.concatenate([-sine, cosine], axis=1)
    return np.concatenate([upper, lower], axis=0)


def twiddle_table():
    indices = np.arange(ROOT)
    angles = (indices[:, None] * indices[None, :]) * (2.0 * math.pi / (ROOT * ROOT))
    return np.stack([np.cos(angles), np.sin(angles)]) / ROOT


def tables():
    quarters = dft_table().reshape(2, ROOT, 2, ROOT).transpose(0, 2, 1, 3).reshape(4, ROOT, ROOT)
    return np.concatenate([twiddle_table(), quarters]).astype(np.float32).reshape(6 * ROOT, ROOT)


def kernel(
    x_ref, tab_ref, out_ref,
    xin, tin, taps, m, wide, frames, hop, turned, snd, mid, rcv,
    acc, acc3, left, mine, sib_snd, sib3_snd, sib_rcv, sib3_rcv, x_snd, x3_snd, x_rcv, x3_rcv,
    d1, d2, d1_snd, d1_rcv, d2_snd, d2_rcv, d1_xs, d1_xr, d2_xs, d2_xr,
    in_sem, const_sem, halo_s, halo_r, hop_s, hop_r, newest_s, newest_r, z_s, z_r, xy_s, xy_r, xl_s, xl_r, loc_sem,
    sib_s, sib_r, x_s, x_r, ds_s, ds_r, dx_s, dx_r,
):
    chan, tm = lax.axis_index("chan"), lax.axis_index("tm")
    x_lo, y, z = chan // 32, (chan // 8) % 4, chan % 8
    x_hi, core = tm // 2, tm % 2
    xy = x_lo * 4 + y
    sibling = x_hi * 2 + 1 - core
    partner = (1 - x_hi) * 2 + core

    def chan_of(xy_, z_):
        return xy_ * 8 + z_

    def other_xy(k):
        return ((x_lo + k // 4) % 2) * 4 + (y + k % 4) % 4

    constants = pltpu.make_async_copy(tab_ref, tin, const_sem.at[0])
    constants.start()
    for i in range(INP):
        pltpu.make_async_copy(x_ref.at[i], xin.at[i], in_sem.at[i]).start()

    barrier = pltpu.get_barrier_semaphore()
    for k in range(1, 8):
        pl.semaphore_signal(barrier, inc=1, device_id={"chan": chan_of(xy, (z + k) % 8)}, device_id_type=MESH)
        pl.semaphore_signal(barrier, inc=1, device_id={"chan": chan_of(other_xy(k), z)}, device_id_type=MESH)
    for k in range(1, 4):
        pl.semaphore_signal(barrier, inc=1, device_id={"tm": (tm + k) % 4}, device_id_type=MESH)
    pl.semaphore_signal(
        barrier, inc=1, device_id={"chan": chan_of(other_xy(4), z), "tm": (tm + 3) % 4}, device_id_type=MESH
    )

    @pl.when(tm == 0)
    def _():
        frames[0:3] = jnp.zeros((3, INP, 2, ROOT, ROOT), BF)

    constants.wait()
    for k in range(4):
        taps[k] = tin[pl.ds(k, ROOT, stride=TAPS), :]
        row, col = k // 2 * ROOT, k % 2 * ROOT
        m[row : row + ROOT, col : col + ROOT] = tin[(6 + k) * ROOT : (7 + k) * ROOT].astype(BF)

    pl.semaphore_wait(barrier, 18)

    def halo(j, rest):
        inputs = slice(INP - HOP, INP) if rest else slice(0, INP - HOP)
        return pltpu.make_async_remote_copy(
            src_ref=frames.at[4 + j, inputs], dst_ref=frames.at[j, inputs],
            send_sem=halo_s.at[rest, j], recv_sem=halo_r.at[rest, j],
            device_id={"tm": (tm + 1) % 4}, device_id_type=MESH,
        )

    def hop_out(j):
        return pltpu.make_async_remote_copy(
            src_ref=frames.at[4 + j, INP - HOP : INP], dst_ref=hop.at[j],
            send_sem=halo_s.at[1, j], recv_sem=hop_r.at[j],
            device_id={"chan": chan_of(other_xy(4), z), "tm": (tm + 1) % 4}, device_id_type=MESH,
        )

    def hop_on(j):
        return pltpu.make_async_remote_copy(
            src_ref=hop.at[j], dst_ref=frames.at[j, INP - HOP : INP],
            send_sem=hop_s.at[j], recv_sem=halo_r.at[1, j],
            device_id={"chan": chan_of(other_xy(4), z)}, device_id_type=MESH,
        )

    def newest(step):
        inputs = pl.ds(step * GROUP, GROUP)
        return pltpu.make_async_remote_copy(
            src_ref=frames.at[6, inputs], dst_ref=frames.at[2, inputs],
            send_sem=newest_s.at[step], recv_sem=newest_r.at[step],
            device_id={"tm": (tm + 1) % 4}, device_id_type=MESH,
        )

    def transform(start, sides):
        for a in range(0, GROUP, 2):
            first = jnp.dot(m[...], jnp.concatenate(sides[a : a + 2], axis=1), preferred_element_type=F32)
            rows = []
            for j in range(2):
                real = first[:ROOT, j * ROOT : (j + 1) * ROOT]
                imag = first[ROOT:, j * ROOT : (j + 1) * ROOT]
                cosine, sine = tin[4 * ROOT : 5 * ROOT], tin[5 * ROOT : 6 * ROOT]
                rows.append(
                    jnp.concatenate(
                        [(real * cosine + imag * sine).astype(BF), (imag * cosine - real * sine).astype(BF)],
                        axis=1,
                    )
                )
            second = lax.dot_general(
                m[...], jnp.concatenate(rows, axis=0), NT, preferred_element_type=F32
            )
            for j in range(2):
                turned[pl.ds(start + a + j, 2 * ROOT, stride=INP), :] = second[:, j * ROOT : (j + 1) * ROOT]

    def pack(s):
        def step(g, carry):
            for v in range(8):
                for p in range(2):
                    for d in range(2):
                        row = pl.multiple_of((p * ROOT + 2 * (g * 8 + v) + d) * INP, INP)
                        lane = (p * 2 + d) * ROOT
                        place = (v, g) if s in Z_FIRST else (g, v)
                        snd[s, place[0], place[1], :, lane : lane + ROOT] = turned[pl.ds(row, INP), :].astype(BF)
            return carry

        lax.fori_loop(0, 8, step, 0)

    def first_spectrum():
        def group(step, carry):
            sides = []
            for j in range(GROUP):
                i = step * GROUP + j
                pltpu.make_async_copy(x_ref.at[i], xin.at[i], in_sem.at[i]).wait()
                parts = []
                for p in range(2):
                    wide[2 * j + p] = xin[i, p].astype(F32)
                    total = None
                    for k in range(TAPS):
                        frame = wide[2 * j + p, pl.ds(k, ROOT, stride=SPEC), :]
                        frames[3 + k, i, p] = frame.astype(BF)
                        total = taps[k] * frame if k == 0 else total + taps[k] * frame
                    parts.append(total.astype(BF))
                sides.append(jnp.concatenate(parts, axis=0))

            @pl.when(tm < 3)
            def _():
                newest(step).start()

            transform(step * GROUP, sides)
            return carry

        lax.fori_loop(0, INP // GROUP, group, 0)

        @pl.when(tm == 1)
        def _():
            hop_out(1).start()
            hop_out(0).start()

        @pl.when((tm == 0) | (tm == 2))
        def _():
            halo(1, 1).start()
            halo(0, 1).start()

        @pl.when(tm < 3)
        def _():
            halo(1, 0).start()
            halo(0, 0).start()

        pack(3)

    def spectrum(s):
        def group(step, carry):
            sides = []
            for j in range(GROUP):
                i = step * GROUP + j
                parts = []
                for p in range(2):
                    total = taps[0] * frames[s, i, p].astype(F32)
                    for k in range(1, TAPS):
                        total = total + taps[k] * frames[s + k, i, p].astype(F32)
                    parts.append(total.astype(BF))
                sides.append(jnp.concatenate(parts, axis=0))
            transform(step * GROUP, sides)
            return carry

        lax.fori_loop(0, INP // GROUP, group, 0)
        pack(s)

    def remote(src, dst, send_sem, recv_sem, to_xy, to_z):
        return pltpu.make_async_remote_copy(
            src_ref=src, dst_ref=dst, send_sem=send_sem, recv_sem=recv_sem,
            device_id={"chan": chan_of(to_xy, to_z)}, device_id_type=MESH,
        )

    def z_copy(s, k):
        to, slot = (z + k) % 8, (11 - k) % 8
        if s in Z_FIRST and k != 4:
            src, dst = snd.at[s, to], mid.at[s, slot]
        elif k != 4:
            src, dst = mid.at[s, :, to], rcv.at[s, slot]
        elif s in Z_FIRST:
            src, dst = mid.at[s, LATE], rcv.at[s, LATE]
        else:
            src, dst = mid.at[s, :, to], rcv.at[s, LATE]
        return remote(src, dst, z_s.at[s, k], z_r.at[s, k], xy, to)

    def xy_copy(s, k):
        to = other_xy(k)
        if s in Z_FIRST:
            src, dst = mid.at[s, 0:LATE, to], rcv.at[s, 0:LATE, xy]
        else:
            src, dst = snd.at[s, to], mid.at[s, xy]
        return remote(src, dst, xy_s.at[s, k], xy_r.at[s, k], to, z)

    def xl_copy(s, k):
        to = other_xy(k)
        return remote(snd.at[s, (z + 4) % 8, to], mid.at[s, LATE, xy], xl_s.at[s, k], xl_r.at[s, k], to, z)

    def z_own(s):
        if s in Z_FIRST:
            return pltpu.make_async_copy(snd.at[s, z], mid.at[s, 3], loc_sem.at[s, 0])
        return pltpu.make_async_copy(mid.at[s, :, z], rcv.at[s, 3], loc_sem.at[s, 0])

    def xy_own(s):
        if s in Z_FIRST:
            return pltpu.make_async_copy(mid.at[s, 0:LATE, xy], rcv.at[s, 0:LATE, xy], loc_sem.at[s, 1])
        return pltpu.make_async_copy(snd.at[s, xy], mid.at[s, xy], loc_sem.at[s, 1])

    def xl_own(s):
        return pltpu.make_async_copy(snd.at[s, (z + 4) % 8, xy], mid.at[s, LATE, xy], loc_sem.at[s, 2])

    early = (3, 5, 2, 6, 1, 7)

    def send_z(s):
        for k in early:
            z_copy(s, k).start()
        z_own(s).start()

    def send_xy(s):
        for k in (5, 7, 6, 4, 2, 1, 3):
            xy_copy(s, k).start()
        xy_own(s).start()

    def send_xl(s):
        for k in range(1, 8):
            xl_copy(s, k).start()
        xl_own(s).start()

    def wait_z(s, some=early):
        for k in some:
            z_copy(s, k).wait_recv()

    def wait_xy(s):
        for k in range(1, 8):
            xy_copy(s, k).wait_recv()
        xy_own(s).wait()

    def wait_xl(s):
        for k in range(1, 8):
            xl_copy(s, k).wait_recv()
        xl_own(s).wait()

    def pass_on():
        @pl.when(tm == 2)
        def _():
            for j in (1, 0):
                hop_out(j).wait_recv()
                hop_on(j).start()

    def arrive(j):
        @pl.when(tm > 0)
        def _():
            if j == 2:
                for step in range(INP // GROUP):
                    newest(step).wait_recv()
            else:
                halo(j, 0).wait_recv()
                halo(j, 1).wait_recv()

    def rows_of(s, owner):
        return rcv[s, 0:LATE, pl.ds(2 * owner, 2)].reshape(ROWS, WIDE)

    def columns_of(s, j):
        if j == 3:
            return rcv[s, 6].reshape(ROOT, WIDE)
        return rcv[s, 2 * j : 2 * j + 2].reshape(256, WIDE)

    def with_swapped(left):
        swapped = jnp.concatenate([left[:, 256:], -left[:, :256]], axis=1)
        return jnp.concatenate([left, swapped], axis=0)

    def times(left, right):
        return lax.dot_general(left, right, NT, preferred_element_type=F32)

    def piece(refs, j):
        return refs[1] if j == 3 else refs[0].at[j]

    def acc_of(owner, j):
        return acc3.at[owner] if j == 3 else acc.at[owner, j]

    def correlate(s, fresh):
        def step(owner, carry):
            left = with_swapped(rows_of(s, owner))
            for j in range(4):
                both = times(left, columns_of(s, j))
                if fresh:
                    acc_of(owner, j)[...] = both
                else:
                    acc_of(owner, j)[...] += both
            return carry

        lax.fori_loop(0, 4, step, 0)

    first_spectrum()
    send_z(3)
    arrive(2)
    mine[LATE] = jnp.zeros((512, ROOT), F32)
    spectrum(2)
    send_z(2)
    pass_on()
    arrive(1)
    spectrum(1)
    wait_z(3)
    z_own(3).wait()
    send_xy(3)
    send_z(1)
    arrive(0)
    spectrum(0)
    send_xy(0)
    wait_z(2)
    z_own(2).wait()
    send_xy(2)
    wait_xy(0)
    send_z(0)
    for s in (3, 2, 1):
        send_xl(s)
    wait_xy(3)
    correlate(3, True)
    wait_z(1)
    z_own(1).wait()
    send_xy(1)
    wait_xy(2)
    correlate(2, False)
    for s in (3, 2, 1):
        wait_xl(s)
    wait_xy(1)
    wait_z(0, early[4:])
    for s in (3, 2, 1, 0):
        z_copy(s, 4).start()
    wait_z(0, early[:4])
    z_own(0).wait()

    factor = 1.0 / 4096.0

    def part_of(refs, h, j):
        return refs[1].at[h] if j == 3 else refs[0].at[h, j]

    def sib_copy(h, j):
        return pltpu.make_async_remote_copy(
            src_ref=part_of((sib_snd, sib3_snd), h, j), dst_ref=part_of((sib_rcv, sib3_rcv), h, j),
            send_sem=sib_s.at[h, j], recv_sem=sib_r.at[h, j],
            device_id={"tm": sibling}, device_id_type=MESH,
        )

    def x_copy(j):
        return pltpu.make_async_remote_copy(
            src_ref=piece((x_snd, x3_snd), j), dst_ref=piece((x_rcv, x3_rcv), j),
            send_sem=x_s.at[j], recv_sem=x_r.at[j],
            device_id={"tm": partner}, device_id_type=MESH,
        )

    def block(owner, side, j):
        last = times(left[side, 0], columns_of(0, j)) + times(left[side, 1], columns_of(1, j))
        return (acc_of(owner, j)[...] + last) * factor

    def store_mine(j, both):
        for part in range(2):
            rows = both[part * ROWS : part * ROWS + ROWS]
            mine[2 * j, part * 256 : part * 256 + ROWS] = rows[:, :ROOT]
            if j < 3:
                mine[2 * j + 1, part * 256 : part * 256 + ROWS] = rows[:, ROOT:]

    for h, hi in ((0, 1 - x_hi), (1, x_hi)):
        given, kept = hi * 2 + 1 - core, hi * 2 + core
        for s in range(2):
            left[0, s] = with_swapped(rows_of(s, given))
            left[1, s] = with_swapped(rows_of(s, kept))

        def give(j):
            both = block(given, 0, j)
            part_of((sib_snd, sib3_snd), h, j)[...] = both.astype(BF)
            sib_copy(h, j).start()

        def keep(j):
            both = block(kept, 1, j)
            sib_copy(h, j).wait_recv()
            both = both + part_of((sib_rcv, sib3_rcv), h, j)[...].astype(F32)
            if h == 0:
                piece((x_snd, x3_snd), j)[...] = both.astype(BF)
                x_copy(j).start()
            else:
                store_mine(j, both)

        give(0)
        give(1)
        keep(0)
        give(2)
        keep(1)
        give(3)
        keep(2)
        keep(3)

    def late_part(s, fresh):
        z_copy(s, 4).wait_recv()
        tail = rcv[s, LATE].reshape(ROOT, WIDE)
        tail_both = with_swapped(tail)

        def column(o, carry):
            both = times(with_swapped(rows_of(s, o)), tail)
            if fresh:
                d1[o] = both
            else:
                d1[o] += both
            return carry

        lax.fori_loop(0, 4, column, 0)

        def row(j, carry):
            both = times(tail_both, rcv[s, pl.ds(2 * j, 2)].reshape(256, WIDE))
            if fresh:
                d2[j] = both
            else:
                d2[j] += both
            return carry

        lax.fori_loop(0, 4, row, 0)

    late_part(3, True)
    late_part(2, False)
    late_part(1, False)
    late_part(0, False)

    def d_rows(owner):
        re = d2[:, pl.ds(pl.multiple_of(owner * 32, 32), 32), :]
        im = d2[:, pl.ds(pl.multiple_of(owner * 32 + 128, 32), 32), :]
        return re * factor, im * factor

    def ds_copies(h):
        return [
            pltpu.make_async_remote_copy(
                src_ref=d1_snd.at[h], dst_ref=d1_rcv.at[h], send_sem=ds_s.at[h, 0], recv_sem=ds_r.at[h, 0],
                device_id={"tm": sibling}, device_id_type=MESH,
            ),
            pltpu.make_async_remote_copy(
                src_ref=d2_snd.at[h], dst_ref=d2_rcv.at[h], send_sem=ds_s.at[h, 1], recv_sem=ds_r.at[h, 1],
                device_id={"tm": sibling}, device_id_type=MESH,
            ),
        ]

    dx_copies = [
        pltpu.make_async_remote_copy(
            src_ref=d1_xs, dst_ref=d1_xr, send_sem=dx_s.at[0], recv_sem=dx_r.at[0],
            device_id={"tm": partner}, device_id_type=MESH,
        ),
        pltpu.make_async_remote_copy(
            src_ref=d2_xs, dst_ref=d2_xr, send_sem=dx_s.at[1], recv_sem=dx_r.at[1],
            device_id={"tm": partner}, device_id_type=MESH,
        ),
    ]

    def give_late(h, owner):
        d1_snd[h] = (d1[owner] * factor).astype(BF)
        ds_copies(h)[0].start()
        re, im = d_rows(owner)
        d2_snd[h, 0] = re.astype(BF)
        d2_snd[h, 1] = im.astype(BF)
        ds_copies(h)[1].start()

    give_late(0, (1 - x_hi) * 2 + 1 - core)
    owner = (1 - x_hi) * 2 + core
    ds_copies(0)[0].wait_recv()
    d1_xs[...] = (d1[owner] * factor + d1_rcv[0].astype(F32)).astype(BF)
    dx_copies[0].start()
    re, im = d_rows(owner)
    ds_copies(0)[1].wait_recv()
    d2_xs[0] = (re + d2_rcv[0, 0].astype(F32)).astype(BF)
    d2_xs[1] = (im + d2_rcv[0, 1].astype(F32)).astype(BF)
    dx_copies[1].start()
    give_late(1, x_hi * 2 + 1 - core)

    turn = (z + 5) % 8
    block_of = lax.broadcasted_iota(jnp.int32, (32, ROOT), 1) // INP

    def transposed(tiles):
        for bit in (1, 2, 4):
            low = block_of // bit % 2 == 0
            swapped = list(tiles)
            for a in range(8):
                if a & bit == 0:
                    one, two = tiles[a], tiles[a | bit]
                    swapped[a] = jnp.where(low, one, pltpu.roll(two, bit * INP, 1))
                    swapped[a | bit] = jnp.where(low, pltpu.roll(one, ROOT - bit * INP, 1), two)
            tiles = swapped
        return tiles

    for j in range(4):
        x_copy(j).wait_recv()
        for part in range(2):
            rows = piece((x_rcv, x3_rcv), j)[part * ROWS : part * ROWS + ROWS].astype(F32)
            mine[2 * j, part * 256 : part * 256 + ROWS] += rows[:, :ROOT]
            if j < 3:
                mine[2 * j + 1, part * 256 : part * 256 + ROWS] += rows[:, ROOT:]

    def place(part, t):
        at = pl.ds(pl.multiple_of(part * 256 + t * 32, 32), 32)
        tiles = transposed([mine[(g + 8 - turn) % 8, at, :] for g in range(8)])
        for v in range(2):
            to = pl.ds(pl.multiple_of(v * ROOT + (turn + t) % 8 * INP, INP), INP)
            for c in range(8):
                out_ref[to, part * 1024 + c * ROOT : part * 1024 + c * ROOT + ROOT] = tiles[c][v * INP : v * INP + INP]

    def place_early(t, carry):
        for part in range(2):
            place(part, t)
        return carry

    lax.fori_loop(0, LATE, place_early, 0)

    owner = x_hi * 2 + core
    for copy in ds_copies(1):
        copy.wait_recv()
    own_rows = d_rows(owner)
    dx_copies[0].wait_recv()

    last = (z + 4) % 8

    def place_columns(t, carry):
        for part in range(2):
            at = pl.ds(pl.multiple_of(part * ROWS + t * 32, 32), 32)
            both = d1[owner, at] * factor + d1_rcv[1, at].astype(F32) + d1_xr[at].astype(F32)
            both = pltpu.roll(both, last * INP, 1)
            for c in range(8):
                moved = both if c == 0 else pltpu.roll(both, ROOT - c * INP, 1)
                cols = slice(part * 1024 + c * ROOT, part * 1024 + c * ROOT + ROOT)
                for v in range(2):
                    to = pl.ds(pl.multiple_of(v * ROOT + (turn + t) % 8 * INP, INP), INP)
                    out_ref[to, cols] = jnp.where(
                        block_of[:INP] == last, moved[v * INP : v * INP + INP], out_ref[to, cols]
                    )
        return carry

    lax.fori_loop(0, LATE, place_columns, 0)

    dx_copies[1].wait_recv()
    for part in range(2):
        rows = own_rows[part] + d2_rcv[1, part].astype(F32) + d2_xr[part].astype(F32)
        for t in range(8):
            mine[t, part * 256 + ROWS : part * 256 + 256] = rows[t // 2, :, t % 2 * ROOT : t % 2 * ROOT + ROOT]
        place(part, LATE)

    for s in range(SPEC):
        for k in range(1, 8):
            z_copy(s, k).wait_send()
            xy_copy(s, k).wait_send()
    for s in Z_FIRST:
        for k in range(1, 8):
            xl_copy(s, k).wait_send()
    for j in range(4):
        sib_copy(0, j).wait_send()
        sib_copy(1, j).wait_send()
        x_copy(j).wait_send()
    for h in range(2):
        for copy in ds_copies(h):
            copy.wait_send()
    for copy in dx_copies:
        copy.wait_send()

    @pl.when(tm < 3)
    def _():
        for j in range(2):
            halo(j, 0).wait_send()
            halo(j, 1).wait_send()
        for step in range(INP // GROUP):
            newest(step).wait_send()

    @pl.when(tm == 2)
    def _():
        for j in range(2):
            hop_on(j).wait_send()


def body(samples, filter_taps):
    x = samples.reshape(INP, 2, SPEC, ROOT, ROOT).transpose(0, 1, 3, 2, 4).reshape(INP, 2, SPEC * ROOT, ROOT)
    t = filter_taps.reshape(TAPS, ROOT, ROOT).transpose(1, 0, 2).reshape(TAPS * ROOT, ROOT)
    vmem = pl.BlockSpec(memory_space=pltpu.VMEM)
    hbm = pl.BlockSpec(memory_space=pl.ANY)
    dma = pltpu.SemaphoreType.DMA
    out = pl.pallas_call(
        kernel,
        out_shape=jax.ShapeDtypeStruct((256, 2048), F32),
        in_specs=[hbm, hbm],
        out_specs=vmem,
        scratch_shapes=[
            pltpu.VMEM((INP, 2, SPEC * ROOT, ROOT), BF),
            pltpu.VMEM((10 * ROOT, ROOT), F32),
            pltpu.VMEM((TAPS, ROOT, ROOT), F32),
            pltpu.VMEM((2 * ROOT, 2 * ROOT), BF),
            pltpu.VMEM((2 * GROUP, SPEC * ROOT, ROOT), F32),
            pltpu.VMEM((7, INP, 2, ROOT, ROOT), BF),
            pltpu.VMEM((2, HOP, 2, ROOT, ROOT), BF),
            pltpu.VMEM((2 * ROOT * INP, ROOT), F32),
            pltpu.VMEM((SPEC, 8, 8, INP, WIDE), BF),
            pltpu.VMEM((SPEC, 8, 8, INP, WIDE), BF),
            pltpu.VMEM((SPEC, 8, 8, INP, WIDE), BF),
            pltpu.VMEM((4, 3, 2 * ROWS, 256), F32),
            pltpu.VMEM((4, 2 * ROWS, ROOT), F32),
            pltpu.VMEM((2, 2, 2 * ROWS, WIDE), BF),
            pltpu.VMEM((8, 512, ROOT), F32),
            pltpu.VMEM((2, 3, 2 * ROWS, 256), BF),
            pltpu.VMEM((2, 2 * ROWS, ROOT), BF),
            pltpu.VMEM((2, 3, 2 * ROWS, 256), BF),
            pltpu.VMEM((2, 2 * ROWS, ROOT), BF),
            pltpu.VMEM((3, 2 * ROWS, 256), BF),
            pltpu.VMEM((2 * ROWS, ROOT), BF),
            pltpu.VMEM((3, 2 * ROWS, 256), BF),
            pltpu.VMEM((2 * ROWS, ROOT), BF),
            pltpu.VMEM((4, 2 * ROWS, ROOT), F32),
            pltpu.VMEM((4, 256, 256), F32),
            pltpu.VMEM((2, 2 * ROWS, ROOT), BF),
            pltpu.VMEM((2, 2 * ROWS, ROOT), BF),
            pltpu.VMEM((2, 2, 4, 32, 256), BF),
            pltpu.VMEM((2, 2, 4, 32, 256), BF),
            pltpu.VMEM((2 * ROWS, ROOT), BF),
            pltpu.VMEM((2 * ROWS, ROOT), BF),
            pltpu.VMEM((2, 4, 32, 256), BF),
            pltpu.VMEM((2, 4, 32, 256), BF),
            dma((INP,)), dma((1,)), dma((2, 2)), dma((2, 2)), dma((2,)), dma((2,)),
            dma((INP // GROUP,)), dma((INP // GROUP,)),
            dma((SPEC, 8)), dma((SPEC, 8)),
            dma((SPEC, 8)), dma((SPEC, 8)),
            dma((SPEC, 8)), dma((SPEC, 8)),
            dma((SPEC, 3)),
            dma((2, 4)), dma((2, 4)), dma((4,)), dma((4,)),
            dma((2, 2)), dma((2, 2)), dma((2,)), dma((2,)),
        ],
        compiler_params=pltpu.CompilerParams(
            collective_id=0, has_side_effects=True, vmem_limit_bytes=50 * 2**20
        ),
    )(x, jnp.concatenate([t, jnp.asarray(tables())]))
    return out[None]


def solution(mesh):
    placed = (P("chan", None, "tm", None), P())
    return jax.shard_map(
        body, mesh=mesh, in_specs=placed, out_specs=P("chan", "tm", None), check_vma=False
    )
```

```python
import math

import jax
import jax.numpy as jnp
import numpy as np
from jax import lax
from jax.experimental import pallas as pl
from jax.experimental.pallas import tpu as pltpu
from jax.sharding import PartitionSpec as P

ROOT = 128
TAPS = 4
SPEC = 4
INP = 16
GROUP = 4
HOP = 2
WIDE = 4 * ROOT
LATE = 7
ROWS = LATE * 2 * INP
Z_FIRST = (3, 2, 1)
MESH = pl.DeviceIdType.MESH
BF = jnp.bfloat16
F32 = jnp.float32
NT = (((1,), (1,)), ((), ()))


def dft_table():
    indices = np.arange(ROOT)
    angles = (indices[:, None] * indices[None, :] % ROOT) * (2.0 * math.pi / ROOT)
    cosine, sine = np.cos(angles), np.sin(angles)
    upper = np.concatenate([cosine, sine], axis=1)
    lower = np.concatenate([-sine, cosine], axis=1)
    return np.concatenate([upper, lower], axis=0)


def twiddle_table():
    indices = np.arange(ROOT)
    angles = (indices[:, None] * indices[None, :]) * (2.0 * math.pi / (ROOT * ROOT))
    return np.stack([np.cos(angles), np.sin(angles)]) / ROOT


def tables():
    quarters = dft_table().reshape(2, ROOT, 2, ROOT).transpose(0, 2, 1, 3).reshape(4, ROOT, ROOT)
    return np.concatenate([twiddle_table(), quarters]).astype(np.float32).reshape(6 * ROOT, ROOT)


def kernel(
    x_ref, tab_ref, out_ref,
    xin, tin, taps, m, wide, frames, hop, turned, snd, mid, rcv,
    acc, acc3, left, mine, sib_snd, sib3_snd, sib_rcv, sib3_rcv, x_snd, x3_snd, x_rcv, x3_rcv,
    d1, d2, d1_snd, d1_rcv, d2_snd, d2_rcv, d1_xs, d1_xr, d2_xs, d2_xr,
    in_sem, const_sem, halo_s, halo_r, hop_s, hop_r, newest_s, newest_r, z_s, z_r, xy_s, xy_r, xl_s, xl_r, loc_sem,
    sib_s, sib_r, x_s, x_r, ds_s, ds_r, dx_s, dx_r,
):
    chan, tm = lax.axis_index("chan"), lax.axis_index("tm")
    x_lo, y, z = chan // 32, (chan // 8) % 4, chan % 8
    x_hi, core = tm // 2, tm % 2
    xy = x_lo * 4 + y
    sibling = x_hi * 2 + 1 - core
    partner = (1 - x_hi) * 2 + core

    def chan_of(xy_, z_):
        return xy_ * 8 + z_

    def other_xy(k):
        return ((x_lo + k // 4) % 2) * 4 + (y + k % 4) % 4

    constants = pltpu.make_async_copy(tab_ref, tin, const_sem.at[0])
    constants.start()
    for i in range(INP):
        pltpu.make_async_copy(x_ref.at[i], xin.at[i], in_sem.at[i]).start()

    barrier = pltpu.get_barrier_semaphore()
    for k in range(1, 8):
        pl.semaphore_signal(barrier, inc=1, device_id={"chan": chan_of(xy, (z + k) % 8)}, device_id_type=MESH)
        pl.semaphore_signal(barrier, inc=1, device_id={"chan": chan_of(other_xy(k), z)}, device_id_type=MESH)
    for k in range(1, 4):
        pl.semaphore_signal(barrier, inc=1, device_id={"tm": (tm + k) % 4}, device_id_type=MESH)
    pl.semaphore_signal(
        barrier, inc=1, device_id={"chan": chan_of(other_xy(4), z), "tm": (tm + 3) % 4}, device_id_type=MESH
    )

    @pl.when(tm == 0)
    def _():
        frames[0:3] = jnp.zeros((3, INP, 2, ROOT, ROOT), BF)

    constants.wait()
    for k in range(4):
        taps[k] = tin[pl.ds(k, ROOT, stride=TAPS), :]
        row, col = k // 2 * ROOT, k % 2 * ROOT
        m[row : row + ROOT, col : col + ROOT] = tin[(6 + k) * ROOT : (7 + k) * ROOT].astype(BF)

    pl.semaphore_wait(barrier, 18)

    def halo(j, rest):
        inputs = slice(INP - HOP, INP) if rest else slice(0, INP - HOP)
        return pltpu.make_async_remote_copy(
            src_ref=frames.at[4 + j, inputs], dst_ref=frames.at[j, inputs],
            send_sem=halo_s.at[rest, j], recv_sem=halo_r.at[rest, j],
            device_id={"tm": (tm + 1) % 4}, device_id_type=MESH,
        )

    def hop_out(j):
        return pltpu.make_async_remote_copy(
            src_ref=frames.at[4 + j, INP - HOP : INP], dst_ref=hop.at[j],
            send_sem=halo_s.at[1, j], recv_sem=hop_r.at[j],
            device_id={"chan": chan_of(other_xy(4), z), "tm": (tm + 1) % 4}, device_id_type=MESH,
        )

    def hop_on(j):
        return pltpu.make_async_remote_copy(
            src_ref=hop.at[j], dst_ref=frames.at[j, INP - HOP : INP],
            send_sem=hop_s.at[j], recv_sem=halo_r.at[1, j],
            device_id={"chan": chan_of(other_xy(4), z)}, device_id_type=MESH,
        )

    def newest(step):
        inputs = pl.ds(step * GROUP, GROUP)
        return pltpu.make_async_remote_copy(
            src_ref=frames.at[6, inputs], dst_ref=frames.at[2, inputs],
            send_sem=newest_s.at[step], recv_sem=newest_r.at[step],
            device_id={"tm": (tm + 1) % 4}, device_id_type=MESH,
        )

    def transform(start, sides):
        for a in range(0, GROUP, 2):
            first = jnp.dot(m[...], jnp.concatenate(sides[a : a + 2], axis=1), preferred_element_type=F32)
            rows = []
            for j in range(2):
                real = first[:ROOT, j * ROOT : (j + 1) * ROOT]
                imag = first[ROOT:, j * ROOT : (j + 1) * ROOT]
                cosine, sine = tin[4 * ROOT : 5 * ROOT], tin[5 * ROOT : 6 * ROOT]
                rows.append(
                    jnp.concatenate(
                        [(real * cosine + imag * sine).astype(BF), (imag * cosine - real * sine).astype(BF)],
                        axis=1,
                    )
                )
            second = lax.dot_general(
                m[...], jnp.concatenate(rows, axis=0), NT, preferred_element_type=F32
            )
            for j in range(2):
                turned[pl.ds(start + a + j, 2 * ROOT, stride=INP), :] = second[:, j * ROOT : (j + 1) * ROOT]

    def pack(s):
        def step(g, carry):
            for v in range(8):
                for p in range(2):
                    for d in range(2):
                        row = pl.multiple_of((p * ROOT + 2 * (g * 8 + v) + d) * INP, INP)
                        lane = (p * 2 + d) * ROOT
                        place = (v, g) if s in Z_FIRST else (g, v)
                        snd[s, place[0], place[1], :, lane : lane + ROOT] = turned[pl.ds(row, INP), :].astype(BF)
            return carry

        lax.fori_loop(0, 8, step, 0)

    def first_spectrum():
        def group(step, carry):
            sides = []
            for j in range(GROUP):
                i = step * GROUP + j
                pltpu.make_async_copy(x_ref.at[i], xin.at[i], in_sem.at[i]).wait()
                parts = []
                for p in range(2):
                    wide[2 * j + p] = xin[i, p].astype(F32)
                    total = None
                    for k in range(TAPS):
                        frame = wide[2 * j + p, pl.ds(k, ROOT, stride=SPEC), :]
                        frames[3 + k, i, p] = frame.astype(BF)
                        total = taps[k] * frame if k == 0 else total + taps[k] * frame
                    parts.append(total.astype(BF))
                sides.append(jnp.concatenate(parts, axis=0))

            @pl.when(tm < 3)
            def _():
                newest(step).start()

            transform(step * GROUP, sides)
            return carry

        lax.fori_loop(0, INP // GROUP, group, 0)

        @pl.when(tm == 1)
        def _():
            hop_out(1).start()
            hop_out(0).start()

        @pl.when((tm == 0) | (tm == 2))
        def _():
            halo(1, 1).start()
            halo(0, 1).start()

        @pl.when(tm < 3)
        def _():
            halo(1, 0).start()
            halo(0, 0).start()

        pack(3)

    def spectrum(s):
        def group(step, carry):
            sides = []
            for j in range(GROUP):
                i = step * GROUP + j
                parts = []
                for p in range(2):
                    total = taps[0] * frames[s, i, p].astype(F32)
                    for k in range(1, TAPS):
                        total = total + taps[k] * frames[s + k, i, p].astype(F32)
                    parts.append(total.astype(BF))
                sides.append(jnp.concatenate(parts, axis=0))
            transform(step * GROUP, sides)
            return carry

        lax.fori_loop(0, INP // GROUP, group, 0)
        pack(s)

    def remote(src, dst, send_sem, recv_sem, to_xy, to_z):
        return pltpu.make_async_remote_copy(
            src_ref=src, dst_ref=dst, send_sem=send_sem, recv_sem=recv_sem,
            device_id={"chan": chan_of(to_xy, to_z)}, device_id_type=MESH,
        )

    def z_copy(s, k):
        to, slot = (z + k) % 8, (11 - k) % 8
        if s in Z_FIRST and k != 4:
            src, dst = snd.at[s, to], mid.at[s, slot]
        elif k != 4:
            src, dst = mid.at[s, :, to], rcv.at[s, slot]
        elif s in Z_FIRST:
            src, dst = mid.at[s, LATE], rcv.at[s, LATE]
        else:
            src, dst = mid.at[s, :, to], rcv.at[s, LATE]
        return remote(src, dst, z_s.at[s, k], z_r.at[s, k], xy, to)

    def xy_copy(s, k):
        to = other_xy(k)
        if s in Z_FIRST:
            src, dst = mid.at[s, 0:LATE, to], rcv.at[s, 0:LATE, xy]
        else:
            src, dst = snd.at[s, to], mid.at[s, xy]
        return remote(src, dst, xy_s.at[s, k], xy_r.at[s, k], to, z)

    def xl_copy(s, k):
        to = other_xy(k)
        return remote(snd.at[s, (z + 4) % 8, to], mid.at[s, LATE, xy], xl_s.at[s, k], xl_r.at[s, k], to, z)

    def z_own(s):
        if s in Z_FIRST:
            return pltpu.make_async_copy(snd.at[s, z], mid.at[s, 3], loc_sem.at[s, 0])
        return pltpu.make_async_copy(mid.at[s, :, z], rcv.at[s, 3], loc_sem.at[s, 0])

    def xy_own(s):
        if s in Z_FIRST:
            return pltpu.make_async_copy(mid.at[s, 0:LATE, xy], rcv.at[s, 0:LATE, xy], loc_sem.at[s, 1])
        return pltpu.make_async_copy(snd.at[s, xy], mid.at[s, xy], loc_sem.at[s, 1])

    def xl_own(s):
        return pltpu.make_async_copy(snd.at[s, (z + 4) % 8, xy], mid.at[s, LATE, xy], loc_sem.at[s, 2])

    early = (3, 5, 2, 6, 1, 7)

    def send_z(s):
        for k in early:
            z_copy(s, k).start()
        z_own(s).start()

    def send_xy(s):
        for k in (5, 7, 6, 4, 2, 1, 3):
            xy_copy(s, k).start()
        xy_own(s).start()

    def send_xl(s):
        for k in range(1, 8):
            xl_copy(s, k).start()
        xl_own(s).start()

    def wait_z(s, some=early):
        for k in some:
            z_copy(s, k).wait_recv()

    def wait_xy(s):
        for k in range(1, 8):
            xy_copy(s, k).wait_recv()
        xy_own(s).wait()

    def wait_xl(s):
        for k in range(1, 8):
            xl_copy(s, k).wait_recv()
        xl_own(s).wait()

    def pass_on():
        @pl.when(tm == 2)
        def _():
            for j in (1, 0):
                hop_out(j).wait_recv()
                hop_on(j).start()

    def arrive(j):
        @pl.when(tm > 0)
        def _():
            if j == 2:
                for step in range(INP // GROUP):
                    newest(step).wait_recv()
            else:
                halo(j, 0).wait_recv()
                halo(j, 1).wait_recv()

    def rows_of(s, owner):
        return rcv[s, 0:LATE, pl.ds(2 * owner, 2)].reshape(ROWS, WIDE)

    def columns_of(s, j):
        if j == 3:
            return rcv[s, 6].reshape(ROOT, WIDE)
        return rcv[s, 2 * j : 2 * j + 2].reshape(256, WIDE)

    def with_swapped(left):
        swapped = jnp.concatenate([left[:, 256:], -left[:, :256]], axis=1)
        return jnp.concatenate([left, swapped], axis=0)

    def times(left, right):
        return lax.dot_general(left, right, NT, preferred_element_type=F32)

    def piece(refs, j):
        return refs[1] if j == 3 else refs[0].at[j]

    def acc_of(owner, j):
        return acc3.at[owner] if j == 3 else acc.at[owner, j]

    def correlate(s, fresh):
        def step(owner, carry):
            left = with_swapped(rows_of(s, owner))
            for j in range(4):
                both = times(left, columns_of(s, j))
                if fresh:
                    acc_of(owner, j)[...] = both
                else:
                    acc_of(owner, j)[...] += both
            return carry

        lax.fori_loop(0, 4, step, 0)

    first_spectrum()
    send_z(3)
    arrive(2)
    mine[LATE] = jnp.zeros((512, ROOT), F32)
    spectrum(2)
    send_z(2)
    pass_on()
    arrive(1)
    spectrum(1)
    wait_z(3)
    z_own(3).wait()
    send_xy(3)
    send_z(1)
    arrive(0)
    spectrum(0)
    send_xy(0)
    wait_z(2)
    z_own(2).wait()
    send_xy(2)
    wait_xy(0)
    send_z(0)
    for s in (3, 2, 1):
        send_xl(s)
    wait_xy(3)
    correlate(3, True)
    wait_z(1)
    z_own(1).wait()
    send_xy(1)
    wait_xy(2)
    correlate(2, False)
    for s in (3, 2, 1):
        wait_xl(s)
    wait_xy(1)
    for side in range(2):
        left[side, 1] = with_swapped(rows_of(1, (1 - x_hi) * 2 + (1 - core if side == 0 else core)))
    wait_z(0, early[4:])
    for s in (3, 2, 1, 0):
        z_copy(s, 4).start()
    wait_z(0, early[:4])
    z_own(0).wait()

    factor = 1.0 / 4096.0

    def part_of(refs, h, j):
        return refs[1].at[h] if j == 3 else refs[0].at[h, j]

    def sib_copy(h, j):
        return pltpu.make_async_remote_copy(
            src_ref=part_of((sib_snd, sib3_snd), h, j), dst_ref=part_of((sib_rcv, sib3_rcv), h, j),
            send_sem=sib_s.at[h, j], recv_sem=sib_r.at[h, j],
            device_id={"tm": sibling}, device_id_type=MESH,
        )

    def x_copy(j):
        return pltpu.make_async_remote_copy(
            src_ref=piece((x_snd, x3_snd), j), dst_ref=piece((x_rcv, x3_rcv), j),
            send_sem=x_s.at[j], recv_sem=x_r.at[j],
            device_id={"tm": partner}, device_id_type=MESH,
        )

    def block(owner, side, j):
        last = times(left[side, 0], columns_of(0, j)) + times(left[side, 1], columns_of(1, j))
        return (acc_of(owner, j)[...] + last) * factor

    def store_mine(j, both):
        for part in range(2):
            rows = both[part * ROWS : part * ROWS + ROWS]
            mine[2 * j, part * 256 : part * 256 + ROWS] = rows[:, :ROOT]
            if j < 3:
                mine[2 * j + 1, part * 256 : part * 256 + ROWS] = rows[:, ROOT:]

    for h, hi in ((0, 1 - x_hi), (1, x_hi)):
        given, kept = hi * 2 + 1 - core, hi * 2 + core
        for s in range(1 if h == 0 else 2):
            left[0, s] = with_swapped(rows_of(s, given))
            left[1, s] = with_swapped(rows_of(s, kept))

        def give(j):
            both = block(given, 0, j)
            part_of((sib_snd, sib3_snd), h, j)[...] = both.astype(BF)
            sib_copy(h, j).start()

        def keep(j):
            both = block(kept, 1, j)
            sib_copy(h, j).wait_recv()
            both = both + part_of((sib_rcv, sib3_rcv), h, j)[...].astype(F32)
            if h == 0:
                piece((x_snd, x3_snd), j)[...] = both.astype(BF)
                x_copy(j).start()
            else:
                store_mine(j, both)

        give(3)
        give(0)
        keep(3)
        give(1)
        keep(0)
        give(2)
        keep(1)
        keep(2)

    def late_part(s, fresh):
        z_copy(s, 4).wait_recv()
        tail = rcv[s, LATE].reshape(ROOT, WIDE)
        tail_both = with_swapped(tail)

        def column(o, carry):
            both = times(with_swapped(rows_of(s, o)), tail)
            if fresh:
                d1[o] = both
            else:
                d1[o] += both
            return carry

        lax.fori_loop(0, 4, column, 0)

        def row(j, carry):
            both = times(tail_both, rcv[s, pl.ds(2 * j, 2)].reshape(256, WIDE))
            if fresh:
                d2[j] = both
            else:
                d2[j] += both
            return carry

        lax.fori_loop(0, 4, row, 0)

    late_part(3, True)
    late_part(2, False)
    late_part(1, False)
    late_part(0, False)

    def d_rows(owner):
        re = d2[:, pl.ds(pl.multiple_of(owner * 32, 32), 32), :]
        im = d2[:, pl.ds(pl.multiple_of(owner * 32 + 128, 32), 32), :]
        return re * factor, im * factor

    def ds_copies(h):
        return [
            pltpu.make_async_remote_copy(
                src_ref=d1_snd.at[h], dst_ref=d1_rcv.at[h], send_sem=ds_s.at[h, 0], recv_sem=ds_r.at[h, 0],
                device_id={"tm": sibling}, device_id_type=MESH,
            ),
            pltpu.make_async_remote_copy(
                src_ref=d2_snd.at[h], dst_ref=d2_rcv.at[h], send_sem=ds_s.at[h, 1], recv_sem=ds_r.at[h, 1],
                device_id={"tm": sibling}, device_id_type=MESH,
            ),
        ]

    dx_copies = [
        pltpu.make_async_remote_copy(
            src_ref=d1_xs, dst_ref=d1_xr, send_sem=dx_s.at[0], recv_sem=dx_r.at[0],
            device_id={"tm": partner}, device_id_type=MESH,
        ),
        pltpu.make_async_remote_copy(
            src_ref=d2_xs, dst_ref=d2_xr, send_sem=dx_s.at[1], recv_sem=dx_r.at[1],
            device_id={"tm": partner}, device_id_type=MESH,
        ),
    ]

    def give_late(h, owner):
        d1_snd[h] = (d1[owner] * factor).astype(BF)
        ds_copies(h)[0].start()
        re, im = d_rows(owner)
        d2_snd[h, 0] = re.astype(BF)
        d2_snd[h, 1] = im.astype(BF)
        ds_copies(h)[1].start()

    give_late(0, (1 - x_hi) * 2 + 1 - core)
    owner = (1 - x_hi) * 2 + core
    ds_copies(0)[0].wait_recv()
    d1_xs[...] = (d1[owner] * factor + d1_rcv[0].astype(F32)).astype(BF)
    dx_copies[0].start()
    re, im = d_rows(owner)
    ds_copies(0)[1].wait_recv()
    d2_xs[0] = (re + d2_rcv[0, 0].astype(F32)).astype(BF)
    d2_xs[1] = (im + d2_rcv[0, 1].astype(F32)).astype(BF)
    dx_copies[1].start()
    give_late(1, x_hi * 2 + 1 - core)

    turn = (z + 5) % 8
    block_of = lax.broadcasted_iota(jnp.int32, (32, ROOT), 1) // INP

    def transposed(tiles):
        for bit in (1, 2, 4):
            low = block_of // bit % 2 == 0
            swapped = list(tiles)
            for a in range(8):
                if a & bit == 0:
                    one, two = tiles[a], tiles[a | bit]
                    swapped[a] = jnp.where(low, one, pltpu.roll(two, bit * INP, 1))
                    swapped[a | bit] = jnp.where(low, pltpu.roll(one, ROOT - bit * INP, 1), two)
            tiles = swapped
        return tiles

    for j in range(4):
        x_copy(j).wait_recv()
        for part in range(2):
            rows = piece((x_rcv, x3_rcv), j)[part * ROWS : part * ROWS + ROWS].astype(F32)
            mine[2 * j, part * 256 : part * 256 + ROWS] += rows[:, :ROOT]
            if j < 3:
                mine[2 * j + 1, part * 256 : part * 256 + ROWS] += rows[:, ROOT:]

    def place(part, t):
        at = pl.ds(pl.multiple_of(part * 256 + t * 32, 32), 32)
        tiles = transposed([mine[(g + 8 - turn) % 8, at, :] for g in range(8)])
        for v in range(2):
            to = pl.ds(pl.multiple_of(v * ROOT + (turn + t) % 8 * INP, INP), INP)
            for c in range(8):
                out_ref[to, part * 1024 + c * ROOT : part * 1024 + c * ROOT + ROOT] = tiles[c][v * INP : v * INP + INP]

    def place_early(t, carry):
        for part in range(2):
            place(part, t)
        return carry

    lax.fori_loop(0, LATE, place_early, 0)

    owner = x_hi * 2 + core
    for copy in ds_copies(1):
        copy.wait_recv()
    own_rows = d_rows(owner)
    dx_copies[0].wait_recv()

    last = (z + 4) % 8

    def place_columns(t, carry):
        for part in range(2):
            at = pl.ds(pl.multiple_of(part * ROWS + t * 32, 32), 32)
            both = d1[owner, at] * factor + d1_rcv[1, at].astype(F32) + d1_xr[at].astype(F32)
            both = pltpu.roll(both, last * INP, 1)
            for c in range(8):
                moved = both if c == 0 else pltpu.roll(both, ROOT - c * INP, 1)
                cols = slice(part * 1024 + c * ROOT, part * 1024 + c * ROOT + ROOT)
                for v in range(2):
                    to = pl.ds(pl.multiple_of(v * ROOT + (turn + t) % 8 * INP, INP), INP)
                    out_ref[to, cols] = jnp.where(
                        block_of[:INP] == last, moved[v * INP : v * INP + INP], out_ref[to, cols]
                    )
        return carry

    lax.fori_loop(0, LATE, place_columns, 0)

    dx_copies[1].wait_recv()
    for part in range(2):
        rows = own_rows[part] + d2_rcv[1, part].astype(F32) + d2_xr[part].astype(F32)
        for t in range(8):
            mine[t, part * 256 + ROWS : part * 256 + 256] = rows[t // 2, :, t % 2 * ROOT : t % 2 * ROOT + ROOT]
        place(part, LATE)

    for s in range(SPEC):
        for k in range(1, 8):
            z_copy(s, k).wait_send()
            xy_copy(s, k).wait_send()
    for s in Z_FIRST:
        for k in range(1, 8):
            xl_copy(s, k).wait_send()
    for j in range(4):
        sib_copy(0, j).wait_send()
        sib_copy(1, j).wait_send()
        x_copy(j).wait_send()
    for h in range(2):
        for copy in ds_copies(h):
            copy.wait_send()
    for copy in dx_copies:
        copy.wait_send()

    @pl.when(tm < 3)
    def _():
        for j in range(2):
            halo(j, 0).wait_send()
            halo(j, 1).wait_send()
        for step in range(INP // GROUP):
            newest(step).wait_send()

    @pl.when(tm == 2)
    def _():
        for j in range(2):
            hop_on(j).wait_send()


def body(samples, filter_taps):
    x = samples.reshape(INP, 2, SPEC, ROOT, ROOT).transpose(0, 1, 3, 2, 4).reshape(INP, 2, SPEC * ROOT, ROOT)
    t = filter_taps.reshape(TAPS, ROOT, ROOT).transpose(1, 0, 2).reshape(TAPS * ROOT, ROOT)
    vmem = pl.BlockSpec(memory_space=pltpu.VMEM)
    hbm = pl.BlockSpec(memory_space=pl.ANY)
    dma = pltpu.SemaphoreType.DMA
    out = pl.pallas_call(
        kernel,
        out_shape=jax.ShapeDtypeStruct((256, 2048), F32),
        in_specs=[hbm, hbm],
        out_specs=vmem,
        scratch_shapes=[
            pltpu.VMEM((INP, 2, SPEC * ROOT, ROOT), BF),
            pltpu.VMEM((10 * ROOT, ROOT), F32),
            pltpu.VMEM((TAPS, ROOT, ROOT), F32),
            pltpu.VMEM((2 * ROOT, 2 * ROOT), BF),
            pltpu.VMEM((2 * GROUP, SPEC * ROOT, ROOT), F32),
            pltpu.VMEM((7, INP, 2, ROOT, ROOT), BF),
            pltpu.VMEM((2, HOP, 2, ROOT, ROOT), BF),
            pltpu.VMEM((2 * ROOT * INP, ROOT), F32),
            pltpu.VMEM((SPEC, 8, 8, INP, WIDE), BF),
            pltpu.VMEM((SPEC, 8, 8, INP, WIDE), BF),
            pltpu.VMEM((SPEC, 8, 8, INP, WIDE), BF),
            pltpu.VMEM((4, 3, 2 * ROWS, 256), F32),
            pltpu.VMEM((4, 2 * ROWS, ROOT), F32),
            pltpu.VMEM((2, 2, 2 * ROWS, WIDE), BF),
            pltpu.VMEM((8, 512, ROOT), F32),
            pltpu.VMEM((2, 3, 2 * ROWS, 256), BF),
            pltpu.VMEM((2, 2 * ROWS, ROOT), BF),
            pltpu.VMEM((2, 3, 2 * ROWS, 256), BF),
            pltpu.VMEM((2, 2 * ROWS, ROOT), BF),
            pltpu.VMEM((3, 2 * ROWS, 256), BF),
            pltpu.VMEM((2 * ROWS, ROOT), BF),
            pltpu.VMEM((3, 2 * ROWS, 256), BF),
            pltpu.VMEM((2 * ROWS, ROOT), BF),
            pltpu.VMEM((4, 2 * ROWS, ROOT), F32),
            pltpu.VMEM((4, 256, 256), F32),
            pltpu.VMEM((2, 2 * ROWS, ROOT), BF),
            pltpu.VMEM((2, 2 * ROWS, ROOT), BF),
            pltpu.VMEM((2, 2, 4, 32, 256), BF),
            pltpu.VMEM((2, 2, 4, 32, 256), BF),
            pltpu.VMEM((2 * ROWS, ROOT), BF),
            pltpu.VMEM((2 * ROWS, ROOT), BF),
            pltpu.VMEM((2, 4, 32, 256), BF),
            pltpu.VMEM((2, 4, 32, 256), BF),
            dma((INP,)), dma((1,)), dma((2, 2)), dma((2, 2)), dma((2,)), dma((2,)),
            dma((INP // GROUP,)), dma((INP // GROUP,)),
            dma((SPEC, 8)), dma((SPEC, 8)),
            dma((SPEC, 8)), dma((SPEC, 8)),
            dma((SPEC, 8)), dma((SPEC, 8)),
            dma((SPEC, 3)),
            dma((2, 4)), dma((2, 4)), dma((4,)), dma((4,)),
            dma((2, 2)), dma((2, 2)), dma((2,)), dma((2,)),
        ],
        compiler_params=pltpu.CompilerParams(
            collective_id=0, has_side_effects=True, vmem_limit_bytes=50 * 2**20
        ),
    )(x, jnp.concatenate([t, jnp.asarray(tables())]))
    return out[None]


def solution(mesh):
    placed = (P("chan", None, "tm", None), P())
    return jax.shard_map(
        body, mesh=mesh, in_specs=placed, out_specs=P("chan", "tm", None), check_vma=False
    )
```
